256 devices in a mesh: seq: 32 (over x, z_lo, core), head: 8 (over y, z_hi).
Axes of the slice: x: 4, y: 4, z: 8 (z_hi: 2, z_lo: 4; z = z_hi * 4 + z_lo), core: 2. Of those that a mesh axis runs over, the one named last changes fastest.
Arguments:
- tokens: bfloat16 [20480, 6144], P('seq'), may hold values from -6 to 6
- w_qkv: bfloat16 [3, 6144, 4096], P(None, 'seq', 'head'), may hold values from -0.07782233 to 0.07782233
- log_decay: float32 [32, 20480], P('head', 'seq'), may hold values from -0.7 to 0, as said below
- gain: float32 [4096], P('head'), may hold values from 0.5 to 1.5
Outputs:
- normed: bfloat16 [20480, 4096], P('seq', 'head')
The draws below stay inside these ranges and needn't reach their ends.
Inputs may be any that keep to these rules, and one draw needn't show every extreme that they name: `log_decay`: every entry is negative.
All inputs are finite; a program needn't handle non-finite values.
Results may differ from the reference program's by a relative error of at most 0.0061.
Values may be sent and summed in bfloat16 or wider, within the bound.
No kernel may reach another device: no remote copies, remote signals or barrier semaphores. Data moves between devices by JAX's collectives and lax.ppermute only.
A program may use at most 128 MiB of HBM per device.

```python
import math
import jax
import jax.numpy as jnp
from jax import lax

D = 6144
HEAD_COUNT = 32
DH = 128
TOK_DEV = 640
TOKEN_COUNT = 20480


def draw_w_qkv(key, part):
    key = jax.random.fold_in(key, 11)
    head_groups = jax.random.split(key, 1)
    width = HEAD_COUNT * DH
    column = jnp.arange(width).astype(jnp.float32) / (width - 1)
    base = jnp.clip(jax.random.normal(head_groups[0], (3, D, width)), -3.0, 3.0)
    rising = 1.0 + column
    factor = jnp.stack([jnp.ones((width,), jnp.float32), jnp.ones((width,), jnp.float32), rising])
    return (base * factor[:, None, :] * D ** (-0.5)).astype(jnp.bfloat16)


def draw_log_decay(key, part):
    key = jax.random.fold_in(key, 23)
    head_groups = jax.random.split(key, 7)
    share = 0.5
    quick_heads = jax.random.uniform(head_groups[0], (HEAD_COUNT,)) < share
    quick_rate = jnp.exp(jax.random.uniform(head_groups[1], (HEAD_COUNT,), minval=math.log(1.0 / 50.0), maxval=math.log(1.0 / 30.0)))
    slow_rate = jnp.exp(jax.random.uniform(head_groups[2], (HEAD_COUNT,), minval=math.log(0.1), maxval=math.log(0.5))) / TOKEN_COUNT
    base_rate = jnp.where(quick_heads, quick_rate, slow_rate)
    sections = TOKEN_COUNT // TOK_DEV
    section_factor = jnp.exp(jax.random.uniform(head_groups[3], (HEAD_COUNT, sections), minval=math.log(0.5), maxval=math.log(2.0)))
    section_factor = jnp.repeat(section_factor, TOK_DEV, axis=1)
    roughness = jax.random.uniform(head_groups[4], (HEAD_COUNT, TOKEN_COUNT), minval=0.5, maxval=1.5)
    block_starts = jax.random.randint(head_groups[5], (3,), 0, TOKEN_COUNT)
    token_offset = jnp.arange(TOKEN_COUNT)
    block_tokens = jnp.any(token_offset[None, :] == block_starts[:, None], axis=0)
    block_length = jax.random.uniform(head_groups[6], (HEAD_COUNT, TOKEN_COUNT), minval=math.log(0.5), maxval=math.log(0.8))
    within_block = -base_rate[:, None] * section_factor * roughness
    return jnp.where(block_tokens[None, :], block_length, within_block).astype(jnp.float32)


def levels(stream_key, extent, shards, smallest, top_value):
    def one(dim, blocks):
        steps = jax.random.uniform(jax.random.fold_in(jax.random.fold_in(stream_key, 6), dim), (blocks,), jnp.float32, smallest / len(shards), top_value / len(shards))
        return jnp.repeat(jnp.exp(steps), extent[dim] // blocks).reshape((-1,) + (1,) * (len(extent) - dim - 1))

    level = one(*shards[0])
    for cut in shards[1:]:
        level = level * one(*cut)
    return level


def scatter_about(own_key, dims, scale, limit, shards=(), dtype=jnp.bfloat16):
    array = scale * jax.random.normal(own_key, dims, jnp.float32)
    if shards:
        array = array * levels(own_key, dims, shards, -0.22, 0.18)
    return jnp.clip(array, -limit, limit).astype(dtype)


def setup_inputs(seed: int = 0) -> dict:
    streams_of = jax.random.split(jax.random.key(seed), 5)
    return {
        "tokens": scatter_about(streams_of[0], (TOKEN_COUNT, D), 1.0, 6.0, ((0, 32),)),
        "w_qkv": draw_w_qkv(jax.random.fold_in(streams_of[4], 71), 0),
        "log_decay": draw_log_decay(jax.random.fold_in(streams_of[4], 71), 0),
        "gain": jnp.clip(1.0 + 0.1 * jax.random.normal(streams_of[3], (HEAD_COUNT * DH,), jnp.float32), 0.5, 1.5),
    }


def section_out(block, decay, state, w_qkv):
    scale = DH ** (-0.5)
    parts = [jnp.dot(block, w_qkv[c], preferred_element_type=jnp.float32).astype(jnp.bfloat16).reshape(TOK_DEV, HEAD_COUNT, DH) for c in range(3)]
    queries, key_rows, value_rows = parts
    cumulative = jnp.cumsum(decay, axis=1)
    total = cumulative[:, -1]
    token_offset = jnp.arange(TOK_DEV)
    causal = token_offset[:, None] >= token_offset[None, :]
    gap = cumulative[:, :, None] - cumulative[:, None, :]
    decay_mask = jnp.exp(jnp.where(causal[None, :, :], gap, -1e+30))
    raw = jnp.einsum('ihd,jhd->hij', queries.astype(jnp.float32), key_rows.astype(jnp.float32))
    probs = (raw * scale * decay_mask).astype(jnp.bfloat16)
    intra = jnp.einsum('hij,jhd->ihd', probs.astype(jnp.float32), value_rows.astype(jnp.float32))
    tail = jnp.exp(total[:, None] - cumulative).T
    scaled_keys = (key_rows.astype(jnp.float32) * tail[:, :, None]).astype(jnp.bfloat16)
    local_state = jnp.einsum('thd,the->hde', scaled_keys.astype(jnp.float32), value_rows.astype(jnp.float32))
    inter = jnp.einsum('thd,hde->the', queries.astype(jnp.float32), state, precision=lax.Precision.HIGHEST)
    attended = intra + inter * (jnp.exp(cumulative).T * scale)[:, :, None]
    new_state = jnp.exp(total)[:, None, None] * state + local_state
    return (attended, new_state)

def reference(tokens, w_qkv, log_decay, gain):
    sections = TOKEN_COUNT // TOK_DEV
    token_blocks = tokens.reshape(sections, TOK_DEV, D)
    decay_blocks = log_decay.reshape(HEAD_COUNT, sections, TOK_DEV).transpose(1, 0, 2)
    gains = gain.reshape(HEAD_COUNT, DH)

    def advance(state, inputs):
        block, decay = inputs
        attended, new_state = section_out(block, decay, state, w_qkv)
        mean_square = lax.optimization_barrier(jnp.mean(attended * attended, axis=(1, 2)))
        normed = attended * lax.rsqrt(mean_square + 1e-06)[:, None, None] * gains[None, :, :]
        return (new_state, normed.astype(jnp.bfloat16).reshape(TOK_DEV, HEAD_COUNT * DH))
    start = jnp.zeros((HEAD_COUNT, DH, DH), jnp.float32)
    final_state, outputs = lax.scan(advance, start, (token_blocks, decay_blocks))
    return outputs.reshape(TOKEN_COUNT, HEAD_COUNT * DH)
```

```python
import functools

import jax
import jax.numpy as jnp
from jax import lax
from jax.experimental import pallas as pl
from jax.experimental.pallas import tpu as pltpu
from jax.sharding import Mesh, PartitionSpec as P

HEAD_COUNT = 32
DH = 128
F32, BF16 = jnp.float32, jnp.bfloat16
NEXT = [(i, (i + 1) % 4) for i in range(4)]
LAST = [(i, (i - 1) % 4) for i in range(4)]
SWAP = [(0, 1), (1, 0)]
VMEM_LIMIT = 48 * 1024 * 1024


def tied(value, *others):
    return lax.optimization_barrier((value, others))[0]


def gather_round(own):
    half = own.shape[0] // 2
    slots, opposite = [], None
    for distance in range(4):
        if distance:
            own = lax.ppermute(own, "zl", NEXT)
        right, left = lax.ppermute(own, "x", NEXT), lax.ppermute(own, "x", LAST)
        if distance in (1, 2):
            opposite = lax.ppermute(opposite, "zl", NEXT)
        else:
            opposite = jnp.concatenate([lax.ppermute(right[:half], "x", NEXT), lax.ppermute(left[half:], "x", LAST)])
        slots.append((own, right, left, opposite))
    return slots


def project_body(count, first, last, index_ref, *refs):
    blocks, rest = refs[:8], refs[8:]
    weights = [ref[...] for ref in rest[:4]]
    acc_ref, out_ref = (None, rest[4]) if first else (rest[4], rest[5])
    for place in range(2):
        rows = jnp.concatenate([ref[...] for ref in blocks[4 * place : 4 * place + 4]], axis=1)
        for c in range(count):
            w = jnp.concatenate([part[c] for part in weights], axis=0)
            total = jnp.dot(rows, w, preferred_element_type=F32)
            if not first:
                total += acc_ref[place, c]
            out_ref[place, c] = total.astype(out_ref.dtype)


def project(index, mine, theirs, weights, acc, last):
    count, depth, width = weights[0].shape
    rows = mine.shape[0]
    tile = rows // 2
    token_specs = [pl.BlockSpec((tile, depth), functools.partial(lambda n, i, ref: (i, ref[n]), n)) for n in range(4)]
    weight_specs = [pl.BlockSpec((count, depth, width), lambda i, ref: (0, 0, 0))] * 4
    acc_spec = pl.BlockSpec((2, count, tile, width), lambda i, ref: (0, 0, i, 0))
    first = acc is None
    return pl.pallas_call(
        functools.partial(project_body, count, first, last),
        out_shape=jax.ShapeDtypeStruct((2, count, rows, width), BF16 if last else F32),
        grid_spec=pltpu.PrefetchScalarGridSpec(
            num_scalar_prefetch=1,
            grid=(2,),
            in_specs=token_specs * 2 + weight_specs + ([] if first else [acc_spec]),
            out_specs=acc_spec,
        ),
        compiler_params=pltpu.CompilerParams(vmem_limit_bytes=VMEM_LIMIT),
        cost_estimate=pl.CostEstimate(
            flops=16 * rows * depth * count * width, bytes_accessed=16 * rows * depth, transcendentals=0
        ),
    )(index, *([mine] * 4), *([theirs] * 4), *weights, *([] if first else [acc]))


def join(earlier, later):
    return jnp.exp(later[1])[:, None, :] * earlier[0] + later[0], earlier[1] + later[1]


def unpack(ref, mask=None):
    state, total = ref[:, :DH, :], ref[:, DH, :]
    if mask is not None:
        state, total = state * mask, total * mask
    return state, total


def pack(ref, value):
    ref[:, :DH, :] = value[0]
    ref[:, DH:, :] = jnp.broadcast_to(value[1][:, None, :], (ref.shape[0], 8, DH))


def state_body(place_ref, kv_ref, tail_ref, total_ref, chip_ref, first_ref):
    group = chip_ref.shape[0]
    second_mine = place_ref[0].astype(F32)
    for h in range(group):
        cut = slice(h * DH, (h + 1) * DH)
        local = []
        for place in range(2):
            keys = (kv_ref[place, 0, :, cut].astype(F32) * tail_ref[place, h]).astype(BF16)
            local.append(
                lax.dot_general(keys, kv_ref[place, 1, :, cut], (((0,), (0,)), ((), ())), preferred_element_type=F32)
            )
        mine, theirs = (local[0], total_ref[0, h]), (local[1], total_ref[1, h])
        first = [jnp.where(second_mine > 0, b, a) for a, b in zip(mine, theirs)]
        second = [jnp.where(second_mine > 0, a, b) for a, b in zip(mine, theirs)]
        first_ref[h, :DH, :] = first[0]
        first_ref[h, DH:, :] = jnp.broadcast_to(first[1], (8, DH))
        chip_ref[h, :DH, :] = jnp.exp(second[1]) * first[0] + second[0]
        chip_ref[h, DH:, :] = jnp.broadcast_to(first[1] + second[1], (8, DH))


def row_body(z_ref, own_ref, back1, back2, back3, before_ref, row_ref):
    z = z_ref[0]
    backs = [back1, back2, back3]
    before = [unpack(ref, (j + 1 <= z).astype(F32)) for j, ref in enumerate(backs)]
    after = [unpack(ref, (j + 1 > z).astype(F32)) for j, ref in enumerate(backs)]
    prefix = join(join(before[2], before[1]), before[0])
    suffix = join(join(after[2], after[1]), after[0])
    pack(before_ref, prefix)
    pack(row_ref, join(join(prefix, unpack(own_ref)), suffix))


def incoming_body(place_ref, before_ref, first_ref, back1, back2, back3, out_ref):
    rows = join(join(unpack(back3), unpack(back2)), unpack(back1))
    state = join(rows, unpack(before_ref))[0]
    first = unpack(first_ref)
    later = jnp.exp(first[1])[:, None, :] * state + first[0]
    mine_second = place_ref[0].astype(F32)
    out_ref[0] = jnp.where(mine_second > 0, later, state)
    out_ref[1] = jnp.where(mine_second > 0, state, later)


def small_kernel(body, out_shapes, scalar, *args):
    return pl.pallas_call(
        body,
        out_shape=[jax.ShapeDtypeStruct(s, F32) for s in out_shapes],
        in_specs=[pl.BlockSpec(memory_space=pltpu.SMEM)] + [pl.BlockSpec(memory_space=pltpu.VMEM)] * len(args),
        out_specs=[pl.BlockSpec(memory_space=pltpu.VMEM)] * len(out_shapes),
        compiler_params=pltpu.CompilerParams(vmem_limit_bytes=VMEM_LIMIT),
    )(scalar, *args)


def attend_body(scale, q_ref, k_ref, v_ref, column_ref, row_ref, state_ref, out_ref, square_ref):
    rows = q_ref.shape[2]
    q, k, v = q_ref[0, 0], k_ref[0, 0], v_ref[0, 0]
    column, row = column_ref[0, 0], row_ref[0, 0]
    inter = jnp.dot(q.astype(F32), state_ref[0, 0], precision=lax.Precision.HIGHEST, preferred_element_type=F32)
    grown = jnp.exp(column) * scale
    for start in range(0, rows, DH):
        stop = start + DH
        raw = lax.dot_general(q[start:stop], k[:stop], (((1,), (1,)), ((), ())), preferred_element_type=F32)
        gap = column[start:stop] - row[:, :stop]
        causal = start + lax.broadcasted_iota(jnp.int32, gap.shape, 0) >= lax.broadcasted_iota(jnp.int32, gap.shape, 1)
        mask = jnp.exp(jnp.where(causal, gap, -1e30))
        scores = (raw * scale * mask).astype(BF16)
        intra = jnp.dot(scores, v[:stop], preferred_element_type=F32)
        attended = intra + inter[start:stop] * grown[start:stop]
        out_ref[0, start:stop, :] = attended
        squares = lax.dot_general(
            jnp.ones((8, DH), F32),
            attended * attended,
            (((1,), (1,)), ((), ())),
            precision=lax.Precision.HIGHEST,
            preferred_element_type=F32,
        )
        square_ref[0, 0, :, start:stop] = squares


def attend(q, kv, column, row, state):
    _, _, rows, width = q.shape
    group = width // DH
    q_spec = pl.BlockSpec((1, 1, rows, DH), lambda a, h: (a, 0, 0, h))
    v_spec = pl.BlockSpec((1, 1, rows, DH), lambda a, h: (a, 1, 0, h))
    return pl.pallas_call(
        functools.partial(attend_body, DH**-0.5),
        out_shape=[
            jax.ShapeDtypeStruct((2, rows, width), F32),
            jax.ShapeDtypeStruct((2, group, 8, rows), F32),
        ],
        grid=(2, group),
        in_specs=[
            q_spec,
            q_spec,
            v_spec,
            pl.BlockSpec((1, 1, rows, 1), lambda a, h: (a, h, 0, 0)),
            pl.BlockSpec((1, 1, 1, rows), lambda a, h: (a, h, 0, 0)),
            pl.BlockSpec((1, 1, DH, DH), lambda a, h: (a, h, 0, 0)),
        ],
        out_specs=[
            pl.BlockSpec((1, rows, DH), lambda a, h: (a, 0, h)),
            pl.BlockSpec((1, 1, 8, rows), lambda a, h: (a, h, 0, 0)),
        ],
        compiler_params=pltpu.CompilerParams(vmem_limit_bytes=VMEM_LIMIT),
    )(q, kv, kv, column, row, state)


def on_device(tokens, w_qkv, log_decay, gain):
    rows = tokens.shape[0]
    width = w_qkv.shape[2] // 2
    group = width // DH
    x, z, core = lax.axis_index("x"), lax.axis_index("zl"), lax.axis_index("core")
    place = core.reshape(1)

    def halves(array, axis):
        size = array.shape[axis] // 2
        mine = lax.dynamic_slice_in_dim(array, core * size, size, axis)
        theirs = lax.dynamic_slice_in_dim(array, (1 - core) * size, size, axis)
        return mine, theirs

    kept, sent = halves(w_qkv, 2)
    got = lax.ppermute(sent, "core", SWAP)
    own = jnp.where(core == 0, jnp.concatenate([kept, got], 1), jnp.concatenate([got, kept], 1))
    kept, sent = halves(log_decay, 0)
    decay = jnp.stack([kept, lax.ppermute(tied(sent, own), "core", SWAP)])
    other_tokens = lax.ppermute(tied(tokens, own), "core", SWAP)

    cumulative = jnp.cumsum(decay, axis=2)
    total = cumulative[:, :, -1]
    tail = jnp.exp(total[:, :, None] - cumulative)[..., None]
    totals = jnp.broadcast_to(total[:, :, None, None], (2, group, 1, DH))

    columns = jnp.stack([x, (x + 3) % 4, (x + 1) % 4, (x + 2) % 4])
    index = [(4 * columns + (z + 4 - d) % 4).astype(jnp.int32) for d in range(4)]

    kv_slots = gather_round(own[1:])
    q_slots = gather_round(own[0].reshape(2, -1, width))
    kv = None
    for d in range(4):
        kv = project(index[d], tokens, other_tokens, kv_slots[d], kv, d == 3)

    shape = (group, DH + 8, DH)
    chip, first = small_kernel(state_body, [shape, shape], place, kv, tail, totals)
    backs = [lax.ppermute(chip, "zl", [(i, (i + j) % 4) for i in range(4)]) for j in (1, 2, 3)]
    before, row = small_kernel(row_body, [shape, shape], z.reshape(1), chip, *backs)
    backs = [lax.ppermute(row, "x", [(i, i + j) for i in range(4 - j)]) for j in (1, 2, 3)]
    (state,) = small_kernel(incoming_body, [(2, group, DH, DH)], place, before, first, *backs)

    q = None
    for d in range(4):
        parts = [part.reshape(1, -1, width) for part in q_slots[d]]
        q = project(index[d], tokens, other_tokens, parts, q, d == 3)

    attended, squares = attend(q, kv, cumulative[..., None], cumulative[:, :, None, :], state)
    squares = jnp.sum(squares[:, :, 0, :], axis=1)
    got = lax.ppermute(attended[1], "core", SWAP)
    summed = squares[0] + lax.ppermute(squares[1], "core", SWAP)
    head_ring = [(a, b) for a in range(4) for b in range(2)]
    others = []
    for dy in range(4):
        for dz in range(2):
            if dy or dz:
                pairs = [(2 * a + b, 2 * ((a + dy) % 4) + (b + dz) % 2) for a, b in head_ring]
                others.append(lax.ppermute(summed, ("y", "zh"), pairs))
    summed = summed + sum(others)
    scale = lax.rsqrt(summed / (HEAD_COUNT * DH) + 1e-6)[:, None]
    mine = attended[0]
    whole = jnp.where(core == 0, jnp.concatenate([mine, got], 1), jnp.concatenate([got, mine], 1))
    return (whole * scale * gain[None, :]).astype(BF16)


def solution(mesh):
    fine = Mesh(mesh.devices.reshape(4, 4, 2, 4, 2), ("x", "zl", "core", "y", "zh"))
    seq, head = ("x", "zl", "core"), ("y", "zh")
    return jax.shard_map(
        on_device,
        mesh=fine,
        in_specs=(P(seq, None), P(None, seq, head), P(head, seq), P(head)),
        out_specs=P(seq, head),
        check_vma=False,
    )
```

```python
import functools

import jax
import jax.numpy as jnp
from jax import lax
from jax.experimental import pallas as pl
from jax.experimental.pallas import tpu as pltpu
from jax.sharding import Mesh, PartitionSpec as P

HEAD_COUNT = 32
DH = 128
TAIL = 16
F32, BF16 = jnp.float32, jnp.bfloat16
NEXT = [(i, (i + 1) % 4) for i in range(4)]
LAST = [(i, (i - 1) % 4) for i in range(4)]
SWAP = [(0, 1), (1, 0)]
VMEM_LIMIT = 48 * 1024 * 1024


def tied(value, *others):
    return lax.optimization_barrier((value, others))[0]


def gather_kv(own):
    half = own.shape[0] // 2
    slots, opposite = [], None
    for distance in range(4):
        if distance:
            own = lax.ppermute(own, "zl", NEXT)
        right, left = lax.ppermute(own, "x", NEXT), lax.ppermute(own, "x", LAST)
        if distance in (1, 2):
            opposite = lax.ppermute(opposite, "zl", NEXT)
        else:
            opposite = jnp.concatenate([lax.ppermute(right[:half], "x", NEXT), lax.ppermute(left[half:], "x", LAST)])
        slots.append((own, right, left, opposite))
    return slots


def gather_q(own):
    columns = [own]
    for _ in range(3):
        columns.append(lax.ppermute(columns[-1], "zl", NEXT))
    column = jnp.concatenate(columns)
    half = column.shape[0] // 2
    right, left = lax.ppermute(column, "x", NEXT), lax.ppermute(column, "x", LAST)
    return [column, right, left], [lax.ppermute(right[:half], "x", NEXT), lax.ppermute(left[half:], "x", LAST)]


def project_body(count, chunks, parts, has_acc, index_ref, *refs):
    mine, theirs, weights = refs[:chunks], refs[chunks : 2 * chunks], refs[2 * chunks : 2 * chunks + parts]
    out_ref = refs[-1]
    tile = mine[0].shape[0]
    rows = jnp.concatenate(
        [jnp.concatenate([ref[...] for ref in mine], axis=1), jnp.concatenate([ref[...] for ref in theirs], axis=1)], axis=0
    )
    for c in range(count):
        cuts = [ref.shape[0] // count for ref in weights]
        w = jnp.concatenate([ref[c * cut : (c + 1) * cut, :] for ref, cut in zip(weights, cuts)], axis=0)
        total = jnp.dot(rows, w, preferred_element_type=F32)
        for place in range(2):
            part = total[place * tile : (place + 1) * tile]
            if has_acc:
                part = part + refs[-2][place, c]
            out_ref[place, c] = part.astype(out_ref.dtype)


def project(count, depth, index, mine, theirs, weights, acc, last):
    rows, width = mine.shape[0], weights[0].shape[1]
    tile, chunks, parts = rows // 4, len(index), len(weights)
    token_specs = [pl.BlockSpec((tile, depth), functools.partial(lambda n, i, ref: (i, ref[n]), n)) for n in range(chunks)]
    weight_specs = [pl.BlockSpec(part.shape, lambda i, ref: (0, 0)) for part in weights]
    acc_spec = pl.BlockSpec((2, count, tile, width), lambda i, ref: (0, 0, i, 0))
    return pl.pallas_call(
        functools.partial(project_body, count, chunks, parts, acc is not None),
        out_shape=jax.ShapeDtypeStruct((2, count, rows, width), BF16 if last else F32),
        grid_spec=pltpu.PrefetchScalarGridSpec(
            num_scalar_prefetch=1,
            grid=(4,),
            in_specs=token_specs * 2 + weight_specs + ([] if acc is None else [acc_spec]),
            out_specs=acc_spec,
        ),
        compiler_params=pltpu.CompilerParams(vmem_limit_bytes=VMEM_LIMIT),
        cost_estimate=pl.CostEstimate(
            flops=4 * rows * depth * chunks * count * width, bytes_accessed=4 * rows * depth * chunks, transcendentals=0
        ),
    )(jnp.stack(index), *([mine] * chunks), *([theirs] * chunks), *weights, *([] if acc is None else [acc]))


def join(earlier, later):
    return jnp.exp(later[1])[:, None, :] * earlier[0] + later[0], earlier[1] + later[1]


def split(value, count):
    parts = []
    for _ in range(count):
        parts.append(value.astype(BF16).astype(F32))
        value = value - parts[-1]
    return parts


def unpack(ref, mask=None):
    state, total = ref[:, :DH, :].astype(F32), jnp.sum(ref[:, DH:, :].astype(F32), axis=1)
    if mask is not None:
        state, total = state * mask, total * mask
    return state, total


def pack(ref, value):
    ref[:, :DH, :] = value[0].astype(ref.dtype)
    row = lax.broadcasted_iota(jnp.int32, (ref.shape[0], TAIL, DH), 1)
    tail = jnp.zeros(row.shape, F32)
    for n, part in enumerate(split(value[1], 3)):
        tail = jnp.where(row == n, part[:, None, :], tail)
    ref[:, DH:, :] = tail.astype(ref.dtype)


def state_body(place_ref, kv_ref, column_ref, total_ref, chip_ref, sent_ref, first_ref):
    group = chip_ref.shape[0]
    second_mine = place_ref[0].astype(F32)
    states, totals = [], []
    for place in range(2):
        total = jnp.stack([total_ref[place, h, 0] for h in range(group)])
        local = []
        for h in range(group):
            cut = slice(h * DH, (h + 1) * DH)
            decay = jnp.exp(total[h : h + 1, :1] - column_ref[place, h])
            keys = (kv_ref[place, 0, :, cut].astype(F32) * decay).astype(BF16)
            local.append(
                lax.dot_general(keys, kv_ref[place, 1, :, cut], (((0,), (0,)), ((), ())), preferred_element_type=F32)
            )
        states.append(jnp.stack(local))
        totals.append(total)
    first = [jnp.where(second_mine > 0, v[1], v[0]) for v in (states, totals)]
    second = [jnp.where(second_mine > 0, v[0], v[1]) for v in (states, totals)]
    pack(first_ref, first)
    both = join(first, second)
    pack(chip_ref, both)
    pack(sent_ref, both)


def row_body(z_ref, own_ref, back1, back2, back3, before_ref, row_ref):
    z = z_ref[0]
    backs = [back1, back2, back3]
    before = [unpack(ref, (j + 1 <= z).astype(F32)) for j, ref in enumerate(backs)]
    after = [unpack(ref, (j + 1 > z).astype(F32)) for j, ref in enumerate(backs)]
    prefix = join(join(before[2], before[1]), before[0])
    suffix = join(join(after[2], after[1]), after[0])
    pack(before_ref, prefix)
    pack(row_ref, join(join(prefix, unpack(own_ref)), suffix))


def incoming_body(place_ref, before_ref, first_ref, back1, back2, back3, out_ref):
    rows = join(join(unpack(back3), unpack(back2)), unpack(back1))
    state = join(rows, unpack(before_ref))[0]
    first = unpack(first_ref)
    later = jnp.exp(first[1])[:, None, :] * state + first[0]
    mine_second = place_ref[0].astype(F32)
    for place, value in enumerate(
        (jnp.where(mine_second > 0, later, state), jnp.where(mine_second > 0, state, later))
    ):
        for n, part in enumerate(split(value, 3)):
            out_ref[place, :, n * DH : (n + 1) * DH, :] = part.astype(BF16)


def small_kernel(body, outs, scalar, *args):
    return pl.pallas_call(
        body,
        out_shape=[jax.ShapeDtypeStruct(*out) for out in outs],
        in_specs=[pl.BlockSpec(memory_space=pltpu.SMEM)] + [pl.BlockSpec(memory_space=pltpu.VMEM)] * len(args),
        out_specs=[pl.BlockSpec(memory_space=pltpu.VMEM)] * len(outs),
        compiler_params=pltpu.CompilerParams(vmem_limit_bytes=VMEM_LIMIT),
    )(scalar, *args)


def attend_body(scale, q_ref, kv_ref, column_ref, row_ref, state_ref, out_ref, square_ref):
    rows, width = q_ref.shape[2:]
    across = (((1,), (1,)), ((), ()))
    i, j = (lax.broadcasted_iota(jnp.int32, (DH, DH), axis) for axis in range(2))
    ones = jnp.ones((8, DH), BF16)
    for start in range(0, rows, DH):
        stop = start + DH
        squares = jnp.zeros((8, DH), F32)
        for h in range(width // DH):
            cut = slice(h * DH, (h + 1) * DH)
            q = q_ref[0, 0, start:stop, cut]
            column, row = column_ref[0, h, start:stop], row_ref[0, h, :, :stop]
            raw = lax.dot_general(q, kv_ref[0, 0, :stop, cut], across, preferred_element_type=F32) * scale
            gap = jnp.where(i >= j, column - row[:, start:], -1e30)
            scores = (raw[:, start:] * jnp.exp(gap)).astype(BF16)
            if start:
                border = row[:, start - 1 : start]
                faded = raw[:, :start] * jnp.exp(column - border) * jnp.exp(border - row[:, :start])
                scores = jnp.concatenate([faded.astype(BF16), scores], axis=1)
            intra = jnp.dot(scores, kv_ref[0, 1, :stop, cut], preferred_element_type=F32)
            inter = jnp.dot(jnp.concatenate([q] * 3, axis=1), state_ref[0, h], preferred_element_type=F32)
            attended = intra + inter * (jnp.exp(column) * scale)
            out_ref[0, start:stop, cut] = attended
            for part in split(attended * attended, 2):
                squares += lax.dot_general(ones, part.astype(BF16), across, preferred_element_type=F32)
        square_ref[0, :, start:stop] = squares


def attend(q, kv, column, row, state):
    _, _, rows, width = q.shape
    group = width // DH

    def whole(shape):
        return pl.BlockSpec((1,) + shape, lambda a: (a,) + (0,) * len(shape))

    return pl.pallas_call(
        functools.partial(attend_body, DH**-0.5),
        out_shape=[jax.ShapeDtypeStruct((2, rows, width), F32), jax.ShapeDtypeStruct((2, 8, rows), F32)],
        grid=(2,),
        in_specs=[
            whole((1, rows, width)),
            whole((2, rows, width)),
            whole((group, rows, 1)),
            whole((group, 1, rows)),
            whole((group, 3 * DH, DH)),
        ],
        out_specs=[whole((rows, width)), whole((8, rows))],
        compiler_params=pltpu.CompilerParams(vmem_limit_bytes=VMEM_LIMIT),
        cost_estimate=pl.CostEstimate(flops=4 * 10**9, bytes_accessed=6 * 10**6, transcendentals=10**6),
    )(q, kv, column, row, state)


def on_device(tokens, w_qkv, log_decay, gain):
    rows = tokens.shape[0]
    width = w_qkv.shape[2] // 2
    group = width // DH
    x, z, core = lax.axis_index("x"), lax.axis_index("zl"), lax.axis_index("core")
    place = core.reshape(1)

    def halves(array, axis):
        size = array.shape[axis] // 2
        mine = lax.dynamic_slice_in_dim(array, core * size, size, axis)
        theirs = lax.dynamic_slice_in_dim(array, (1 - core) * size, size, axis)
        return mine, theirs

    kept, sent = halves(w_qkv, 2)
    got = lax.ppermute(sent, "core", SWAP)
    own = jnp.where(core == 0, jnp.concatenate([kept, got], 1), jnp.concatenate([got, kept], 1))
    kept, sent = halves(log_decay, 0)
    decay = jnp.stack([kept, lax.ppermute(tied(sent, own), "core", SWAP)])
    other_tokens = lax.ppermute(tied(tokens, own), "core", SWAP)

    cumulative = jnp.cumsum(decay, axis=2)
    column = cumulative[..., None]
    totals = jnp.broadcast_to(cumulative[:, :, -1][:, :, None, None], (2, group, 1, DH))

    columns = [x, (x + 3) % 4, (x + 1) % 4, (x + 2) % 4]
    index = [[(4 * c + (z + 4 - d) % 4).astype(jnp.int32) for d in range(4)] for c in columns]

    depth = own.shape[1]
    slots = gather_kv(own[1:].reshape(2 * depth, width))
    q_early, q_late = gather_q(own[0])
    early = [(d, n) for d in (0, 1) for n in (0, 1, 2)] + [(0, 3)]
    late = [(d, n) for d in range(4) for n in range(4) if (d, n) not in early]
    kv = None
    for some in (early, late):
        chunk = [index[n][d] for d, n in some]
        kv = project(2, depth, chunk, tokens, other_tokens, [slots[d][n] for d, n in some], kv, some is late)

    shape = (group, DH + TAIL, DH)
    chip, sent, first = small_kernel(state_body, [(shape, F32), (shape, BF16), (shape, F32)], place, kv, column, totals)
    backs = [lax.ppermute(sent, "zl", [(i, (i + j) % 4) for i in range(4)]) for j in (1, 2, 3)]
    before, row = small_kernel(row_body, [(shape, F32), (shape, BF16)], z.reshape(1), chip, *backs)
    backs = [lax.ppermute(row, "x", [(i, i + j) for i in range(4 - j)]) for j in (1, 2, 3)]
    (state,) = small_kernel(incoming_body, [((2, group, 3 * DH, DH), BF16)], place, before, first, *backs)

    q = project(1, depth, sum(index[:3], []), tokens, other_tokens, q_early, None, False)
    q = project(1, depth, index[3], tokens, other_tokens, q_late, q, True)

    attended, squares = attend(q, kv, column, cumulative[:, :, None, :], state)
    squares = squares[:, 0, :]
    summed = squares[0] + lax.ppermute(squares[1], "core", SWAP)
    got = lax.ppermute(attended[1], "core", SWAP)
    summed = summed + sum(lax.ppermute(summed, "y", [(i, (i + j) % 4) for i in range(4)]) for j in (1, 2, 3))
    summed = summed + lax.ppermute(summed, "zh", SWAP)
    scale = lax.rsqrt(summed / (HEAD_COUNT * DH) + 1e-6)[:, None]
    mine = attended[0]
    whole = jnp.where(core == 0, jnp.concatenate([mine, got], 1), jnp.concatenate([got, mine], 1))
    return (whole * scale * gain[None, :]).astype(BF16)


def solution(mesh):
    fine = Mesh(mesh.devices.reshape(4, 4, 2, 4, 2), ("x", "zl", "core", "y", "zh"))
    seq, head = ("x", "zl", "core"), ("y", "zh")
    return jax.shard_map(
        on_device,
        mesh=fine,
        in_specs=(P(seq, None), P(None, seq, head), P(head, seq), P(head)),
        out_specs=P(seq, head),
        check_vma=False,
    )
```

```python
import functools

import jax
import jax.numpy as jnp
from jax import lax
from jax.experimental import pallas as pl
from jax.experimental.pallas import tpu as pltpu
from jax.sharding import Mesh, PartitionSpec as P

HEAD_COUNT = 32
DH = 128
TAIL = 16
F32, BF16 = jnp.float32, jnp.bfloat16
NEXT = [(i, (i + 1) % 4) for i in range(4)]
LAST = [(i, (i - 1) % 4) for i in range(4)]
SWAP = [(0, 1), (1, 0)]
VMEM_LIMIT = 48 * 1024 * 1024


ACROSS = (((1,), (1,)), ((), ()))


def tied(value, *others):
    return lax.optimization_barrier((value, others))[0]


def project_body(count, chunks, has_acc, index_ref, *refs):
    mine, theirs, weights = refs[:chunks], refs[chunks : 2 * chunks], refs[2 * chunks : (2 + count) * chunks]
    out_ref = refs[-1]
    tile = mine[0].shape[0]
    rows = jnp.concatenate(
        [jnp.concatenate([ref[...] for ref in mine], axis=1), jnp.concatenate([ref[...] for ref in theirs], axis=1)], axis=0
    )
    for c in range(count):
        w = jnp.concatenate([ref[...] for ref in weights[c * chunks : (c + 1) * chunks]], axis=0)
        total = jnp.dot(rows, w, preferred_element_type=F32)
        for place in range(2):
            part = total[place * tile : (place + 1) * tile]
            if has_acc:
                part = part + refs[-2][place, c]
            out_ref[place, c] = part.astype(out_ref.dtype)


def project(first, count, index, mine, theirs, weights, acc, last):
    rows, width = mine.shape[0], weights[0].shape[1]
    depth = weights[0].shape[0] // 3
    tile, chunks = rows // 4, len(index)
    token_specs = [pl.BlockSpec((tile, depth), functools.partial(lambda n, i, ref: (i, ref[n]), n)) for n in range(chunks)]
    weight_specs = [
        pl.BlockSpec((depth, width), functools.partial(lambda c, i, ref: (c, 0), first + c))
        for c in range(count)
        for _ in range(chunks)
    ]
    acc_spec = pl.BlockSpec((2, count, tile, width), lambda i, ref: (0, 0, i, 0))
    return pl.pallas_call(
        functools.partial(project_body, count, chunks, acc is not None),
        out_shape=jax.ShapeDtypeStruct((2, count, rows, width), BF16 if last else F32),
        grid_spec=pltpu.PrefetchScalarGridSpec(
            num_scalar_prefetch=1,
            grid=(4,),
            in_specs=token_specs * 2 + weight_specs + ([] if acc is None else [acc_spec]),
            out_specs=acc_spec,
        ),
        compiler_params=pltpu.CompilerParams(vmem_limit_bytes=VMEM_LIMIT),
        cost_estimate=pl.CostEstimate(
            flops=4 * rows * depth * chunks * count * width, bytes_accessed=4 * rows * depth * chunks, transcendentals=0
        ),
    )(
        jnp.stack(index),
        *([mine] * chunks),
        *([theirs] * chunks),
        *(list(weights) * count),
        *([] if acc is None else [acc]),
    )


def join(earlier, later):
    return jnp.exp(later[1])[:, None, :] * earlier[0] + later[0], earlier[1] + later[1]


def split(value, count):
    parts = []
    for _ in range(count):
        parts.append(value.astype(BF16).astype(F32))
        value = value - parts[-1]
    return parts


def unpack(ref, mask=None):
    state, total = ref[:, :DH, :].astype(F32), jnp.sum(ref[:, DH:, :].astype(F32), axis=1)
    if mask is not None:
        state, total = state * mask, total * mask
    return state, total


def pack(ref, value):
    ref[:, :DH, :] = value[0].astype(ref.dtype)
    row = lax.broadcasted_iota(jnp.int32, (ref.shape[0], TAIL, DH), 1)
    tail = jnp.zeros(row.shape, F32)
    for n, part in enumerate(split(value[1], 3)):
        tail = jnp.where(row == n, part[:, None, :], tail)
    ref[:, DH:, :] = tail.astype(ref.dtype)


def state_body(place_ref, kv_ref, column_ref, total_ref, chip_ref, sent_ref, first_ref):
    group = chip_ref.shape[0]
    second_mine = place_ref[0].astype(F32)
    states, totals = [], []
    for place in range(2):
        total = jnp.stack([total_ref[place, h, 0] for h in range(group)])
        local = []
        for h in range(group):
            cut = slice(h * DH, (h + 1) * DH)
            decay = jnp.exp(total[h : h + 1, :1] - column_ref[place, h])
            keys = (kv_ref[place, 0, :, cut].astype(F32) * decay).astype(BF16)
            local.append(
                lax.dot_general(keys, kv_ref[place, 1, :, cut], (((0,), (0,)), ((), ())), preferred_element_type=F32)
            )
        states.append(jnp.stack(local))
        totals.append(total)
    first = [jnp.where(second_mine > 0, v[1], v[0]) for v in (states, totals)]
    second = [jnp.where(second_mine > 0, v[0], v[1]) for v in (states, totals)]
    pack(first_ref, first)
    both = join(first, second)
    pack(chip_ref, both)
    pack(sent_ref, both)


def row_body(z_ref, own_ref, back1, back2, back3, before_ref, row_ref):
    z = z_ref[0]
    backs = [back1, back2, back3]
    before = [unpack(ref, (j + 1 <= z).astype(F32)) for j, ref in enumerate(backs)]
    after = [unpack(ref, (j + 1 > z).astype(F32)) for j, ref in enumerate(backs)]
    prefix = join(join(before[2], before[1]), before[0])
    suffix = join(join(after[2], after[1]), after[0])
    pack(before_ref, prefix)
    pack(row_ref, join(join(prefix, unpack(own_ref)), suffix))


def incoming_body(place_ref, before_ref, first_ref, back1, back2, back3, out_ref):
    rows = join(join(unpack(back3), unpack(back2)), unpack(back1))
    state = join(rows, unpack(before_ref))[0]
    first = unpack(first_ref)
    later = jnp.exp(first[1])[:, None, :] * state + first[0]
    mine_second = place_ref[0].astype(F32)
    for place, value in enumerate(
        (jnp.where(mine_second > 0, later, state), jnp.where(mine_second > 0, state, later))
    ):
        for n, part in enumerate(split(value, 3)):
            out_ref[place, :, n * DH : (n + 1) * DH, :] = part.astype(BF16)


def small_kernel(body, outs, scalar, *args):
    return pl.pallas_call(
        body,
        out_shape=[jax.ShapeDtypeStruct(*out) for out in outs],
        in_specs=[pl.BlockSpec(memory_space=pltpu.SMEM)] + [pl.BlockSpec(memory_space=pltpu.VMEM)] * len(args),
        out_specs=[pl.BlockSpec(memory_space=pltpu.VMEM)] * len(outs),
        compiler_params=pltpu.CompilerParams(vmem_limit_bytes=VMEM_LIMIT),
    )(scalar, *args)


def intra_body(scale, q_ref, kv_ref, column_ref, row_ref, out_ref):
    rows, width = q_ref.shape[2:]
    i, j = (lax.broadcasted_iota(jnp.int32, (DH, DH), axis) for axis in range(2))
    for start in range(0, rows, DH):
        stop = start + DH
        for h in range(width // DH):
            cut = slice(h * DH, (h + 1) * DH)
            q = q_ref[0, 0, start:stop, cut]
            column, row = column_ref[0, h, start:stop], row_ref[0, h, :, :stop]
            raw = lax.dot_general(q, kv_ref[0, 0, :stop, cut], ACROSS, preferred_element_type=F32) * scale
            gap = jnp.where(i >= j, column - row[:, start:], -1e30)
            scores = (raw[:, start:] * jnp.exp(gap)).astype(BF16)
            if start:
                border = row[:, start - 1 : start]
                faded = raw[:, :start] * jnp.exp(column - border) * jnp.exp(border - row[:, :start])
                scores = jnp.concatenate([faded.astype(BF16), scores], axis=1)
            out_ref[0, start:stop, cut] = jnp.dot(scores, kv_ref[0, 1, :stop, cut], preferred_element_type=F32)


def inter_body(scale, q_ref, column_ref, intra_ref, state_ref, out_ref, square_ref):
    rows, width = q_ref.shape[2:]
    squares = jnp.zeros((8, rows), F32)
    for h in range(width // DH):
        cut = slice(h * DH, (h + 1) * DH)
        q = q_ref[0, 0, :, cut]
        inter = jnp.dot(jnp.concatenate([q] * 3, axis=1), state_ref[0, h], preferred_element_type=F32)
        attended = intra_ref[0, :, cut] + inter * (jnp.exp(column_ref[0, h]) * scale)
        out_ref[0, :, cut] = attended
        for part in split(attended * attended, 2):
            squares += lax.dot_general(jnp.ones((8, DH), BF16), part.astype(BF16), ACROSS, preferred_element_type=F32)
    square_ref[0] = squares


def by_place(body, outs, flops, *args):
    def whole(shape):
        return pl.BlockSpec((1,) + shape[1:], lambda a: (a,) + (0,) * (len(shape) - 1))

    return pl.pallas_call(
        functools.partial(body, DH**-0.5),
        out_shape=[jax.ShapeDtypeStruct(shape, F32) for shape in outs],
        grid=(2,),
        in_specs=[whole(arg.shape) for arg in args],
        out_specs=[whole(shape) for shape in outs],
        compiler_params=pltpu.CompilerParams(vmem_limit_bytes=VMEM_LIMIT),
        cost_estimate=pl.CostEstimate(flops=flops, bytes_accessed=4 * 10**6, transcendentals=10**6),
    )(*args)


def on_device(tokens, w_qkv, log_decay, gain):
    rows = tokens.shape[0]
    width = w_qkv.shape[2] // 2
    group = width // DH
    x, z, core = lax.axis_index("x"), lax.axis_index("zl"), lax.axis_index("core")
    place = core.reshape(1)

    def halves(array, axis):
        size = array.shape[axis] // 2
        mine = lax.dynamic_slice_in_dim(array, core * size, size, axis)
        theirs = lax.dynamic_slice_in_dim(array, (1 - core) * size, size, axis)
        return mine, theirs

    kept, sent = halves(w_qkv, 2)
    got = lax.ppermute(sent, "core", SWAP)
    own = jnp.where(core == 0, jnp.concatenate([kept, got], 1), jnp.concatenate([got, kept], 1))
    kept, sent = halves(log_decay, 0)
    decay = jnp.stack([kept, lax.ppermute(tied(sent, own), "core", SWAP)])
    other_tokens = lax.ppermute(tied(tokens, own), "core", SWAP)

    cumulative = jnp.cumsum(decay, axis=2)
    column = cumulative[..., None]
    totals = jnp.broadcast_to(cumulative[:, :, -1][:, :, None, None], (2, group, 1, DH))

    columns = [x, (x + 3) % 4, (x + 1) % 4, (x + 2) % 4]
    index = [[(4 * c + (z + 4 - d) % 4).astype(jnp.int32) for d in range(4)] for c in columns]
    own_x, right_x, left_x, far_x = index

    def along_z(part):
        return lax.ppermute(part, "zl", NEXT)

    def to_right(part):
        return lax.ppermute(part, "x", NEXT)

    def to_left(part):
        return lax.ppermute(part, "x", LAST)

    def partial(parts, chunks, acc):
        kv = project(1, 2, chunks, tokens, other_tokens, parts, acc and acc[0], False)
        return kv, project(0, 1, chunks, tokens, other_tokens, parts, acc and acc[1], False)

    step = lax.optimization_barrier
    own = own.reshape(-1, width)
    half = own.shape[0] // 2
    a1, r0, l0 = along_z(own), to_right(own), to_left(own)
    a1, r0, l0, other_tokens, cumulative, column, totals = step((a1, r0, l0, other_tokens, cumulative, column, totals))

    a2, r1, l1, f0, g0 = along_z(a1), to_right(a1), to_left(a1), to_right(r0[:half]), to_left(l0[half:])
    acc = partial([own, a1, r0, l0], [own_x[0], own_x[1], right_x[0], left_x[0]], None)
    a2, r1, l1, f0, g0, acc = step((a2, r1, l1, f0, g0, acc))

    far0 = jnp.concatenate([f0, g0])
    a3, r2, l2 = along_z(a2), to_right(a2), to_left(a2)
    acc = partial([a2, r1, l1, far0], [own_x[2], right_x[1], left_x[1], far_x[0]], acc)
    a3, r2, l2, acc, far0 = step((a3, r2, l2, acc, far0))

    b1, r3, l3 = along_z(far0), to_right(a3), to_left(a3)
    acc = partial([a3, r2, l2], [own_x[3], right_x[2], left_x[2]], acc)
    b1, r3, l3, acc = step((b1, r3, l3, acc))

    b2, f3, g3 = along_z(b1), to_right(r3[:half]), to_left(l3[half:])
    acc = partial([b1, r3, l3], [far_x[1], right_x[3], left_x[3]], acc)
    b2, f3, g3, acc = step((b2, f3, g3, acc))

    last = [b2, jnp.concatenate([f3, g3])], [far_x[2], far_x[3]]
    kv = project(1, 2, last[1], tokens, other_tokens, last[0], acc[0], True)
    shape = (group, DH + TAIL, DH)
    chip, sent, first = small_kernel(state_body, [(shape, F32), (shape, BF16), (shape, F32)], place, kv, column, totals)
    backs = [lax.ppermute(sent, "zl", [(i, (i + j) % 4) for i in range(4)]) for j in (1, 2, 3)]
    q = project(0, 1, last[1], tokens, other_tokens, last[0], tied(acc[1], sent), True)
    before, row = small_kernel(row_body, [(shape, F32), (shape, BF16)], z.reshape(1), chip, *backs)
    row, q = step((row, q))
    backs = [lax.ppermute(row, "x", [(i, i + j) for i in range(4 - j)]) for j in (1, 2, 3)]
    (intra,) = by_place(intra_body, [(2, rows, width)], 4 * 10**9, q, kv, column, cumulative[:, :, None, :])
    backs, intra = step((backs, intra))
    (state,) = small_kernel(incoming_body, [((2, group, 3 * DH, DH), BF16)], place, before, first, *backs)

    attended, squares = by_place(inter_body, [(2, rows, width), (2, 8, rows)], 10**9, q, column, intra, state)
    squares = squares[:, 0, :]
    summed = squares[0] + lax.ppermute(squares[1], "core", SWAP)
    got = lax.ppermute(attended[1], "core", SWAP)
    summed = summed + sum(lax.ppermute(summed, "y", [(i, (i + j) % 4) for i in range(4)]) for j in (1, 2, 3))
    summed = summed + lax.ppermute(summed, "zh", SWAP)
    scale = lax.rsqrt(summed / (HEAD_COUNT * DH) + 1e-6)[:, None]
    mine = attended[0]
    whole = jnp.where(core == 0, jnp.concatenate([mine, got], 1), jnp.concatenate([got, mine], 1))
    return (whole * scale * gain[None, :]).astype(BF16)


def solution(mesh):
    fine = Mesh(mesh.devices.reshape(4, 4, 2, 4, 2), ("x", "zl", "core", "y", "zh"))
    seq, head = ("x", "zl", "core"), ("y", "zh")
    return jax.shard_map(
        on_device,
        mesh=fine,
        in_specs=(P(seq, None), P(None, seq, head), P(head, seq), P(head)),
        out_specs=P(seq, head),
        check_vma=False,
    )
```

```python
import functools

import jax
import jax.numpy as jnp
from jax import lax
from jax.experimental import pallas as pl
from jax.experimental.pallas import tpu as pltpu
from jax.sharding import Mesh, PartitionSpec as P

HEAD_COUNT = 32
DH = 128
TAIL = 16
F32, BF16 = jnp.float32, jnp.bfloat16
NEXT = [(i, (i + 1) % 4) for i in range(4)]
LAST = [(i, (i - 1) % 4) for i in range(4)]
SWAP = [(0, 1), (1, 0)]
VMEM_LIMIT = 48 * 1024 * 1024


ACROSS = (((1,), (1,)), ((), ()))


def tied(value, *others):
    return lax.optimization_barrier((value, others))[0]


def project_body(groups, chunks, has_acc, index_ref, *refs):
    mine, theirs, weights = refs[:chunks], refs[chunks : 2 * chunks], refs[2 * chunks : 3 * chunks]
    accs, outs = refs[3 * chunks : 3 * chunks + len(groups)], refs[-len(groups) :]
    tile, depth = mine[0].shape
    rows = jnp.concatenate(
        [jnp.concatenate([ref[...] for ref in mine], axis=1), jnp.concatenate([ref[...] for ref in theirs], axis=1)], axis=0
    )
    for g, members in enumerate(groups):
        for n, c in enumerate(members):
            w = jnp.concatenate([ref[c * depth : (c + 1) * depth, :] for ref in weights], axis=0)
            total = jnp.dot(rows, w, preferred_element_type=F32)
            for place in range(2):
                part = total[place * tile : (place + 1) * tile]
                outs[g][place, n] = part + accs[g][place, n] if has_acc else part


def project(index, mine, theirs, weights, accs):
    groups = ((0,), (1, 2))
    rows, width = mine.shape[0], weights[0].shape[1]
    depth = weights[0].shape[0] // 3
    tile, chunks = rows // 4, len(index)
    token_specs = [pl.BlockSpec((tile, depth), functools.partial(lambda n, i, ref: (i, ref[n]), n)) for n in range(chunks)]
    weight_specs = [pl.BlockSpec(part.shape, lambda i, ref: (0, 0)) for part in weights]
    out_specs = [pl.BlockSpec((2, len(g), tile, width), lambda i, ref: (0, 0, i, 0)) for g in groups]
    return pl.pallas_call(
        functools.partial(project_body, groups, chunks, accs is not None),
        out_shape=[jax.ShapeDtypeStruct((2, len(g), rows, width), F32) for g in groups],
        grid_spec=pltpu.PrefetchScalarGridSpec(
            num_scalar_prefetch=1,
            grid=(4,),
            in_specs=token_specs * 2 + weight_specs + (out_specs if accs else []),
            out_specs=out_specs,
        ),
        compiler_params=pltpu.CompilerParams(vmem_limit_bytes=VMEM_LIMIT),
        cost_estimate=pl.CostEstimate(
            flops=12 * rows * depth * chunks * width, bytes_accessed=4 * rows * depth * chunks, transcendentals=0
        ),
    )(jnp.stack(index), *([mine] * chunks), *([theirs] * chunks), *weights, *(accs or []))


def join(earlier, later):
    return jnp.exp(later[1])[:, None, :] * earlier[0] + later[0], earlier[1] + later[1]


def split(value, count):
    parts = []
    for _ in range(count):
        parts.append(value.astype(BF16).astype(F32))
        value = value - parts[-1]
    return parts


def unpack(ref, mask=None):
    state, total = ref[:, :DH, :].astype(F32), jnp.sum(ref[:, DH:, :].astype(F32), axis=1)
    if mask is not None:
        state, total = state * mask, total * mask
    return state, total


def pack(ref, value):
    ref[:, :DH, :] = value[0].astype(ref.dtype)
    row = lax.broadcasted_iota(jnp.int32, (ref.shape[0], TAIL, DH), 1)
    tail = jnp.zeros(row.shape, F32)
    for n, part in enumerate(split(value[1], 3)):
        tail = jnp.where(row == n, part[:, None, :], tail)
    ref[:, DH:, :] = tail.astype(ref.dtype)


def close_body(place_ref, mine_ref, theirs_ref, b_ref, f_ref, g_ref, acc_ref, decay_ref, kv_ref, chip_ref, sent_ref, first_ref):
    group, rows, depth = chip_ref.shape[0], mine_ref.shape[0], b_ref.shape[0] // 3
    half = f_ref.shape[0]
    second_mine = place_ref[0].astype(F32)
    k_weights = jnp.concatenate([b_ref[depth : 2 * depth, :], f_ref[depth:, :], g_ref[: 2 * depth - half, :]], axis=0)
    v_weights = jnp.concatenate([b_ref[2 * depth :, :], g_ref[2 * depth - half :, :]], axis=0)
    states, totals = [], []
    for place, ref in enumerate((mine_ref, theirs_ref)):
        k = (acc_ref[place, 0] + jnp.dot(ref[...], k_weights, preferred_element_type=F32)).astype(BF16)
        v = (acc_ref[place, 1] + jnp.dot(ref[...], v_weights, preferred_element_type=F32)).astype(BF16)
        kv_ref[place, 0] = k
        kv_ref[place, 1] = v
        total = decay_ref[place, :, rows - 1 :]
        tail = jnp.transpose(jnp.exp(total - decay_ref[place]))
        local = []
        for h in range(group):
            cut = slice(h * DH, (h + 1) * DH)
            keys = (k[:, cut].astype(F32) * tail[:, h : h + 1]).astype(BF16)
            local.append(lax.dot_general(keys, v[:, cut], (((0,), (0,)), ((), ())), preferred_element_type=F32))
        states.append(jnp.stack(local))
        totals.append(jnp.broadcast_to(total[:group], (group, DH)))
    first = [jnp.where(second_mine > 0, v[1], v[0]) for v in (states, totals)]
    second = [jnp.where(second_mine > 0, v[0], v[1]) for v in (states, totals)]
    pack(first_ref, first)
    both = join(first, second)
    pack(chip_ref, both)
    pack(sent_ref, both)


def row_body(z_ref, own_ref, back1, back2, back3, before_ref, row_ref):
    z = z_ref[0]
    backs = [back1, back2, back3]
    before = [unpack(ref, (j + 1 <= z).astype(F32)) for j, ref in enumerate(backs)]
    after = [unpack(ref, (j + 1 > z).astype(F32)) for j, ref in enumerate(backs)]
    prefix = join(join(before[2], before[1]), before[0])
    suffix = join(join(after[2], after[1]), after[0])
    pack(before_ref, prefix)
    pack(row_ref, join(join(prefix, unpack(own_ref)), suffix))


def incoming_body(place_ref, before_ref, first_ref, back1, back2, back3, out_ref):
    rows = join(join(unpack(back3), unpack(back2)), unpack(back1))
    state = join(rows, unpack(before_ref))[0]
    first = unpack(first_ref)
    later = jnp.exp(first[1])[:, None, :] * state + first[0]
    mine_second = place_ref[0].astype(F32)
    for place, value in enumerate(
        (jnp.where(mine_second > 0, later, state), jnp.where(mine_second > 0, state, later))
    ):
        for n, part in enumerate(split(value, 3)):
            out_ref[place, :, n * DH : (n + 1) * DH, :] = part.astype(BF16)


def small_kernel(body, outs, scalar, *args):
    return pl.pallas_call(
        body,
        out_shape=[jax.ShapeDtypeStruct(*out) for out in outs],
        in_specs=[pl.BlockSpec(memory_space=pltpu.SMEM)] + [pl.BlockSpec(memory_space=pltpu.VMEM)] * len(args),
        out_specs=[pl.BlockSpec(memory_space=pltpu.VMEM)] * len(outs),
        compiler_params=pltpu.CompilerParams(vmem_limit_bytes=VMEM_LIMIT),
    )(scalar, *args)


def intra_body(scale, place_ref, mine_ref, theirs_ref, b_ref, f_ref, acc_ref, kv_ref, decay_ref, q_ref, out_ref):
    rows, width, depth = mine_ref.shape[0], b_ref.shape[1], b_ref.shape[0] // 3
    i, j = (lax.broadcasted_iota(jnp.int32, (DH, DH), axis) for axis in range(2))
    weights = jnp.concatenate([b_ref[:depth, :], f_ref[:depth, :]], axis=0)
    for place, ref in enumerate((mine_ref, theirs_ref)):
        whole = (acc_ref[place, 0] + jnp.dot(ref[...], weights, preferred_element_type=F32)).astype(BF16)
        q_ref[place] = whole
        columns = jnp.transpose(decay_ref[place])
        for start in range(0, rows, DH):
            stop = start + DH
            for h in range(width // DH):
                cut = slice(h * DH, (h + 1) * DH)
                q = whole[start:stop, cut]
                column, row = columns[start:stop, h : h + 1], decay_ref[place, h : h + 1, :stop]
                raw = lax.dot_general(q, kv_ref[place, 0, :stop, cut], ACROSS, preferred_element_type=F32) * scale
                gap = jnp.where(i >= j, column - row[:, start:], -1e30)
                scores = (raw[:, start:] * jnp.exp(gap)).astype(BF16)
                if start:
                    border = row[:, start - 1 : start]
                    faded = raw[:, :start] * jnp.exp(column - border) * jnp.exp(border - row[:, :start])
                    scores = jnp.concatenate([faded.astype(BF16), scores], axis=1)
                out_ref[place, start:stop, cut] = jnp.dot(
                    scores, kv_ref[place, 1, :stop, cut], preferred_element_type=F32
                )


def inter_body(scale, q_ref, decay_ref, intra_ref, state_ref, out_ref, square_ref):
    rows, width = q_ref.shape[1:]
    squares = jnp.zeros((8, rows), F32)
    grown = jnp.transpose(jnp.exp(decay_ref[0]) * scale)
    for h in range(width // DH):
        cut = slice(h * DH, (h + 1) * DH)
        q = q_ref[0, :, cut]
        inter = jnp.dot(jnp.concatenate([q] * 3, axis=1), state_ref[0, h], preferred_element_type=F32)
        attended = intra_ref[0, :, cut] + inter * grown[:, h : h + 1]
        out_ref[0, :, cut] = attended
        for part in split(attended * attended, 2):
            squares += lax.dot_general(jnp.ones((8, DH), BF16), part.astype(BF16), ACROSS, preferred_element_type=F32)
    square_ref[0] = squares


def by_place(body, outs, flops, *args):
    def whole(shape):
        return pl.BlockSpec((1,) + shape[1:], lambda a: (a,) + (0,) * (len(shape) - 1))

    return pl.pallas_call(
        functools.partial(body, DH**-0.5),
        out_shape=[jax.ShapeDtypeStruct(shape, F32) for shape in outs],
        grid=(2,),
        in_specs=[whole(arg.shape) for arg in args],
        out_specs=[whole(shape) for shape in outs],
        compiler_params=pltpu.CompilerParams(vmem_limit_bytes=VMEM_LIMIT),
        cost_estimate=pl.CostEstimate(flops=flops, bytes_accessed=4 * 10**6, transcendentals=10**6),
    )(*args)


def on_device(tokens, w_qkv, log_decay, gain):
    rows = tokens.shape[0]
    width = w_qkv.shape[2] // 2
    group = width // DH
    x, z, core = lax.axis_index("x"), lax.axis_index("zl"), lax.axis_index("core")
    place = core.reshape(1)

    def halves(array, axis):
        size = array.shape[axis] // 2
        mine = lax.dynamic_slice_in_dim(array, core * size, size, axis)
        theirs = lax.dynamic_slice_in_dim(array, (1 - core) * size, size, axis)
        return mine, theirs

    kept, sent = halves(w_qkv, 2)
    got = lax.ppermute(sent, "core", SWAP)
    own = jnp.where(core == 0, jnp.concatenate([kept, got], 1), jnp.concatenate([got, kept], 1))
    kept, sent = halves(log_decay, 0)
    decay = jnp.stack([kept, lax.ppermute(tied(sent, own), "core", SWAP)])
    other_tokens = lax.ppermute(tied(tokens, own), "core", SWAP)

    fades = jnp.pad(jnp.cumsum(decay, axis=2), ((0, 0), (0, 8 - group), (0, 0)))

    columns = [x, (x + 3) % 4, (x + 1) % 4, (x + 2) % 4]
    index = [[(4 * c + (z + 4 - d) % 4).astype(jnp.int32) for d in range(4)] for c in columns]
    own_x, right_x, left_x, far_x = index

    def along_z(part):
        return lax.ppermute(part, "zl", NEXT)

    def to_right(part):
        return lax.ppermute(part, "x", NEXT)

    def to_left(part):
        return lax.ppermute(part, "x", LAST)

    def tokens_at(array, chunks):
        return jnp.concatenate([lax.dynamic_slice_in_dim(array, c * depth, depth, 1) for c in chunks], axis=1)

    step = lax.optimization_barrier
    depth = own.shape[1]
    own = own.reshape(-1, width)
    half = own.shape[0] // 2
    a1, r0, l0 = along_z(own), to_right(own), to_left(own)
    a1, r0, l0, other_tokens, fades = step((a1, r0, l0, other_tokens, fades))

    a2, r1, l1, f0, g0 = along_z(a1), to_right(a1), to_left(a1), to_right(r0[:half]), to_left(l0[half:])
    last = [tokens_at(array, (far_x[2], far_x[3])) for array in (tokens, other_tokens)]
    a2, r1, l1, f0, g0, last = step((a2, r1, l1, f0, g0, last))

    far0 = jnp.concatenate([f0, g0])
    a3, r2, l2 = along_z(a2), to_right(a2), to_left(a2)
    chunks = [own_x[0], own_x[1], right_x[0], left_x[0], own_x[2], right_x[1], left_x[1], far_x[0]]
    acc = project(chunks, tokens, other_tokens, [own, a1, r0, l0, a2, r1, l1, far0], None)
    a3, r2, l2, acc, far0 = step((a3, r2, l2, acc, far0))

    b1, r3, l3 = along_z(far0), to_right(a3), to_left(a3)
    b1, r3, l3 = step((b1, r3, l3))

    b2, f3, g3 = along_z(b1), to_right(r3[:half]), to_left(l3[half:])
    chunks = [own_x[3], right_x[2], left_x[2], far_x[1], right_x[3], left_x[3]]
    q_acc, kv_acc = project(chunks, tokens, other_tokens, [a3, r2, l2, b1, r3, l3], acc)
    b2, f3, g3, q_acc, kv_acc = step((b2, f3, g3, q_acc, kv_acc))

    shape = (group, DH + TAIL, DH)
    outs = [((2, 2, rows, width), BF16), (shape, F32), (shape, BF16), (shape, F32)]
    kv, chip, sent, first = small_kernel(close_body, outs, place, *last, b2, f3, g3, kv_acc, fades)
    backs = [lax.ppermute(sent, "zl", [(i, (i + j) % 4) for i in range(4)]) for j in (1, 2, 3)]
    outs = [((2, rows, width), BF16), ((2, rows, width), F32)]
    q, intra = small_kernel(functools.partial(intra_body, DH**-0.5), outs, place, *last, b2, f3, q_acc, kv, fades)
    before, row = small_kernel(row_body, [(shape, F32), (shape, BF16)], z.reshape(1), chip, *backs)
    backs = [lax.ppermute(row, "x", [(i, i + j) for i in range(4 - j)]) for j in (1, 2, 3)]
    backs, intra = step((backs, intra))
    (state,) = small_kernel(incoming_body, [((2, group, 3 * DH, DH), BF16)], place, before, first, *backs)

    attended, squares = by_place(inter_body, [(2, rows, width), (2, 8, rows)], 10**9, q, fades, intra, state)
    squares = squares[:, 0, :]
    summed = squares[0] + lax.ppermute(squares[1], "core", SWAP)
    got = lax.ppermute(attended[1], "core", SWAP)
    summed = summed + sum(lax.ppermute(summed, "y", [(i, (i + j) % 4) for i in range(4)]) for j in (1, 2, 3))
    summed = summed + lax.ppermute(summed, "zh", SWAP)
    scale = lax.rsqrt(summed / (HEAD_COUNT * DH) + 1e-6)[:, None]
    mine = attended[0]
    whole = jnp.where(core == 0, jnp.concatenate([mine, got], 1), jnp.concatenate([got, mine], 1))
    return (whole * scale * gain[None, :]).astype(BF16)


def solution(mesh):
    fine = Mesh(mesh.devices.reshape(4, 4, 2, 4, 2), ("x", "zl", "core", "y", "zh"))
    seq, head = ("x", "zl", "core"), ("y", "zh")
    return jax.shard_map(
        on_device,
        mesh=fine,
        in_specs=(P(seq, None), P(None, seq, head), P(head, seq), P(head)),
        out_specs=P(seq, head),
        check_vma=False,
    )
```

```python
import functools

import jax
import jax.numpy as jnp
from jax import lax
from jax.experimental import pallas as pl
from jax.experimental.pallas import tpu as pltpu
from jax.sharding import Mesh, PartitionSpec as P

HEAD_COUNT = 32
DH = 128
TAIL = 16
F32, BF16 = jnp.float32, jnp.bfloat16
NEXT = [(i, (i + 1) % 4) for i in range(4)]
LAST = [(i, (i - 1) % 4) for i in range(4)]
SWAP = [(0, 1), (1, 0)]
VMEM_LIMIT = 20 * 1024 * 1024
PROJECT_LIMIT = 54 * 1024 * 1024


ACROSS = (((1,), (1,)), ((), ()))


def tied(value, *others):
    return lax.optimization_barrier((value, others))[0]


def project_body(has_acc, index_ref, mine_ref, theirs_ref, *refs):
    weights, (out_ref, w_ref, x_ref, w_sem, x_sem) = refs[:-5], refs[-5:]
    if has_acc:
        weights, acc_ref = weights[:-1], weights[-1]
    count, tile, chunks = w_ref.shape[0], x_ref.shape[1] // 2, len(weights)
    depth, tiles = weights[0].shape[0] // count, mine_ref.shape[0] // tile

    def weight_copies(c):
        return [
            pltpu.make_async_copy(
                ref.at[pl.ds(c * depth, depth), :], w_ref.at[c, pl.ds(n * depth, depth), :], w_sem.at[c, n]
            )
            for n, ref in enumerate(weights)
        ]

    def token_copies(t):
        slot = lax.rem(t, 2)
        return [
            pltpu.make_async_copy(
                ref.at[pl.ds(pl.multiple_of(t * tile, tile), tile), pl.ds(pl.multiple_of(index_ref[n] * depth, depth), depth)],
                x_ref.at[slot, pl.ds(place * tile, tile), pl.ds(n * depth, depth)],
                x_sem.at[slot, place, n],
            )
            for place, ref in enumerate((mine_ref, theirs_ref))
            for n in range(chunks)
        ]

    for copy in token_copies(0):
        copy.start()
    for c in range(count):
        for copy in weight_copies(c):
            copy.start()

    @pl.loop(0, tiles)
    def _(t):
        @pl.when(t + 1 < tiles)
        def _():
            for copy in token_copies(t + 1):
                copy.start()

        for copy in token_copies(t):
            copy.wait()
        rows = pl.ds(pl.multiple_of(t * tile, tile), tile)
        for c in range(count):

            @pl.when(t == 0)
            def _():
                for copy in weight_copies(c):
                    copy.wait()

            total = jnp.dot(x_ref[lax.rem(t, 2)], w_ref[c], preferred_element_type=F32)
            for place in range(2):
                part = total[place * tile : (place + 1) * tile]
                out_ref[place, c, rows, :] = part + acc_ref[place, c, rows, :] if has_acc else part


def project(index, mine, theirs, weights, acc):
    rows, width = mine.shape[0], weights[0].shape[1]
    depth = weights[0].shape[0] // 3
    tile, chunks = rows // 4, len(index)
    far, near = pl.BlockSpec(memory_space=pltpu.HBM), pl.BlockSpec(memory_space=pltpu.VMEM)
    return pl.pallas_call(
        functools.partial(project_body, acc is not None),
        out_shape=jax.ShapeDtypeStruct((2, 3, rows, width), F32),
        in_specs=[pl.BlockSpec(memory_space=pltpu.SMEM)] + [far] * (2 + chunks) + ([] if acc is None else [near]),
        out_specs=near,
        scratch_shapes=[
            pltpu.VMEM((3, chunks * depth, width), BF16),
            pltpu.VMEM((2, 2 * tile, chunks * depth), BF16),
            pltpu.SemaphoreType.DMA((3, chunks)),
            pltpu.SemaphoreType.DMA((2, 2, chunks)),
        ],
        input_output_aliases={} if acc is None else {3 + chunks: 0},
        compiler_params=pltpu.CompilerParams(vmem_limit_bytes=PROJECT_LIMIT),
        cost_estimate=pl.CostEstimate(
            flops=12 * rows * depth * chunks * width, bytes_accessed=4 * rows * depth * chunks, transcendentals=0
        ),
    )(jnp.stack(index), mine, theirs, *weights, *([] if acc is None else [acc]))


def join(earlier, later):
    return jnp.exp(later[1])[:, None, :] * earlier[0] + later[0], earlier[1] + later[1]


def split(value, count):
    parts = []
    for _ in range(count):
        parts.append(value.astype(BF16).astype(F32))
        value = value - parts[-1]
    return parts


def unpack(ref, mask=None):
    state, total = ref[:, :DH, :].astype(F32), jnp.sum(ref[:, DH:, :].astype(F32), axis=1)
    if mask is not None:
        state, total = state * mask, total * mask
    return state, total


def pack(ref, value):
    ref[:, :DH, :] = value[0].astype(ref.dtype)
    row = lax.broadcasted_iota(jnp.int32, (ref.shape[0], TAIL, DH), 1)
    tail = jnp.zeros(row.shape, F32)
    for n, part in enumerate(split(value[1], 3)):
        tail = jnp.where(row == n, part[:, None, :], tail)
    ref[:, DH:, :] = tail.astype(ref.dtype)


def close_body(place_ref, mine_ref, theirs_ref, b_ref, f_ref, g_ref, acc_ref, decay_ref, kv_ref, chip_ref, sent_ref, first_ref):
    group, rows, depth = chip_ref.shape[0], mine_ref.shape[0], b_ref.shape[0] // 3
    half = f_ref.shape[0]
    second_mine = place_ref[0].astype(F32)
    k_weights = jnp.concatenate([b_ref[depth : 2 * depth, :], f_ref[depth:, :], g_ref[: 2 * depth - half, :]], axis=0)
    v_weights = jnp.concatenate([b_ref[2 * depth :, :], g_ref[2 * depth - half :, :]], axis=0)
    states, totals = [], []
    for place, ref in enumerate((mine_ref, theirs_ref)):
        k = (acc_ref[place, 1] + jnp.dot(ref[...], k_weights, preferred_element_type=F32)).astype(BF16)
        v = (acc_ref[place, 2] + jnp.dot(ref[...], v_weights, preferred_element_type=F32)).astype(BF16)
        kv_ref[place, 0] = k
        kv_ref[place, 1] = v
        total = decay_ref[place, :, rows - 1 :]
        tail = jnp.transpose(jnp.exp(total - decay_ref[place]))
        local = []
        for h in range(group):
            cut = slice(h * DH, (h + 1) * DH)
            keys = (k[:, cut].astype(F32) * tail[:, h : h + 1]).astype(BF16)
            local.append(lax.dot_general(keys, v[:, cut], (((0,), (0,)), ((), ())), preferred_element_type=F32))
        states.append(jnp.stack(local))
        totals.append(jnp.broadcast_to(total[:group], (group, DH)))
    first = [jnp.where(second_mine > 0, v[1], v[0]) for v in (states, totals)]
    second = [jnp.where(second_mine > 0, v[0], v[1]) for v in (states, totals)]
    pack(first_ref, first)
    both = join(first, second)
    pack(chip_ref, both)
    pack(sent_ref, both)


def row_body(z_ref, own_ref, back1, back2, back3, before_ref, row_ref):
    z = z_ref[0]
    backs = [back1, back2, back3]
    before = [unpack(ref, (j + 1 <= z).astype(F32)) for j, ref in enumerate(backs)]
    after = [unpack(ref, (j + 1 > z).astype(F32)) for j, ref in enumerate(backs)]
    prefix = join(join(before[2], before[1]), before[0])
    suffix = join(join(after[2], after[1]), after[0])
    pack(before_ref, prefix)
    pack(row_ref, join(join(prefix, unpack(own_ref)), suffix))


def incoming_body(place_ref, before_ref, first_ref, back1, back2, back3, out_ref):
    rows = join(join(unpack(back3), unpack(back2)), unpack(back1))
    state = join(rows, unpack(before_ref))[0]
    first = unpack(first_ref)
    later = jnp.exp(first[1])[:, None, :] * state + first[0]
    mine_second = place_ref[0].astype(F32)
    for place, value in enumerate(
        (jnp.where(mine_second > 0, later, state), jnp.where(mine_second > 0, state, later))
    ):
        for n, part in enumerate(split(value, 3)):
            out_ref[place, :, n * DH : (n + 1) * DH, :] = part.astype(BF16)


def small_kernel(body, outs, scalar, *args):
    return pl.pallas_call(
        body,
        out_shape=[jax.ShapeDtypeStruct(*out) for out in outs],
        in_specs=[pl.BlockSpec(memory_space=pltpu.SMEM)] + [pl.BlockSpec(memory_space=pltpu.VMEM)] * len(args),
        out_specs=[pl.BlockSpec(memory_space=pltpu.VMEM)] * len(outs),
        compiler_params=pltpu.CompilerParams(vmem_limit_bytes=VMEM_LIMIT),
    )(scalar, *args)


def intra_body(scale, place_ref, mine_ref, theirs_ref, b_ref, f_ref, acc_ref, kv_ref, decay_ref, q_ref, out_ref):
    rows, width, depth = mine_ref.shape[0], b_ref.shape[1], b_ref.shape[0] // 3
    i, j = (lax.broadcasted_iota(jnp.int32, (DH, DH), axis) for axis in range(2))
    weights = jnp.concatenate([b_ref[:depth, :], f_ref[:depth, :]], axis=0)
    for place, ref in enumerate((mine_ref, theirs_ref)):
        whole = (acc_ref[place, 0] + jnp.dot(ref[...], weights, preferred_element_type=F32)).astype(BF16)
        q_ref[place] = whole
        columns = jnp.transpose(decay_ref[place])
        for start in range(0, rows, DH):
            stop = start + DH
            for h in range(width // DH):
                cut = slice(h * DH, (h + 1) * DH)
                q = whole[start:stop, cut]
                column, row = columns[start:stop, h : h + 1], decay_ref[place, h : h + 1, :stop]
                raw = lax.dot_general(q, kv_ref[place, 0, :stop, cut], ACROSS, preferred_element_type=F32) * scale
                gap = jnp.where(i >= j, column - row[:, start:], -1e30)
                scores = (raw[:, start:] * jnp.exp(gap)).astype(BF16)
                if start:
                    border = row[:, start - 1 : start]
                    faded = raw[:, :start] * jnp.exp(column - border) * jnp.exp(border - row[:, :start])
                    scores = jnp.concatenate([faded.astype(BF16), scores], axis=1)
                out_ref[place, start:stop, cut] = jnp.dot(
                    scores, kv_ref[place, 1, :stop, cut], preferred_element_type=F32
                )


def inter_body(scale, q_ref, decay_ref, intra_ref, state_ref, out_ref, square_ref):
    rows, width = q_ref.shape[1:]
    squares = jnp.zeros((8, rows), F32)
    grown = jnp.transpose(jnp.exp(decay_ref[0]) * scale)
    for h in range(width // DH):
        cut = slice(h * DH, (h + 1) * DH)
        q = q_ref[0, :, cut]
        inter = jnp.dot(jnp.concatenate([q] * 3, axis=1), state_ref[0, h], preferred_element_type=F32)
        attended = intra_ref[0, :, cut] + inter * grown[:, h : h + 1]
        out_ref[0, :, cut] = attended
        for part in split(attended * attended, 2):
            squares += lax.dot_general(jnp.ones((8, DH), BF16), part.astype(BF16), ACROSS, preferred_element_type=F32)
    square_ref[0] = squares


def by_place(body, outs, flops, *args):
    def whole(shape):
        return pl.BlockSpec((1,) + shape[1:], lambda a: (a,) + (0,) * (len(shape) - 1))

    return pl.pallas_call(
        functools.partial(body, DH**-0.5),
        out_shape=[jax.ShapeDtypeStruct(shape, F32) for shape in outs],
        grid=(2,),
        in_specs=[whole(arg.shape) for arg in args],
        out_specs=[whole(shape) for shape in outs],
        compiler_params=pltpu.CompilerParams(vmem_limit_bytes=VMEM_LIMIT),
        cost_estimate=pl.CostEstimate(flops=flops, bytes_accessed=4 * 10**6, transcendentals=10**6),
    )(*args)


def on_device(tokens, w_qkv, log_decay, gain):
    rows = tokens.shape[0]
    width = w_qkv.shape[2] // 2
    group = width // DH
    x, z, core = lax.axis_index("x"), lax.axis_index("zl"), lax.axis_index("core")
    place = core.reshape(1)

    def halves(array, axis):
        size = array.shape[axis] // 2
        mine = lax.dynamic_slice_in_dim(array, core * size, size, axis)
        theirs = lax.dynamic_slice_in_dim(array, (1 - core) * size, size, axis)
        return mine, theirs

    kept, sent = halves(w_qkv, 2)
    got = lax.ppermute(sent, "core", SWAP)
    own = jnp.where(core == 0, jnp.concatenate([kept, got], 1), jnp.concatenate([got, kept], 1))
    kept, sent = halves(log_decay, 0)
    decay = jnp.stack([kept, lax.ppermute(tied(sent, own), "core", SWAP)])
    other_tokens = lax.ppermute(tied(tokens, own), "core", SWAP)

    fades = jnp.pad(jnp.cumsum(decay, axis=2), ((0, 0), (0, 8 - group), (0, 0)))

    columns = [x, (x + 3) % 4, (x + 1) % 4, (x + 2) % 4]
    index = [[(4 * c + (z + 4 - d) % 4).astype(jnp.int32) for d in range(4)] for c in columns]
    own_x, right_x, left_x, far_x = index

    def along_z(part):
        return lax.ppermute(part, "zl", NEXT)

    def to_right(part):
        return lax.ppermute(part, "x", NEXT)

    def to_left(part):
        return lax.ppermute(part, "x", LAST)

    def tokens_at(array, chunks):
        return jnp.concatenate([lax.dynamic_slice_in_dim(array, c * depth, depth, 1) for c in chunks], axis=1)

    step = lax.optimization_barrier
    depth = own.shape[1]
    own = own.reshape(-1, width)
    half = own.shape[0] // 2
    a1, r0, l0 = along_z(own), to_right(own), to_left(own)

    a2, r1, l1, f0, g0 = along_z(a1), to_right(a1), to_left(a1), to_right(r0[:half]), to_left(l0[half:])

    held = tied(a2, a1, r0, l0, other_tokens, fades)
    a3, r2, l2 = along_z(held), to_right(held), to_left(held)

    far0 = jnp.concatenate([f0, g0])
    sent_z, sent_x = tied((far0, a3), a2, r1, l1, f0, g0)
    b1, r3, l3 = along_z(sent_z), to_right(sent_x), to_left(sent_x)
    chunks = [own_x[0], own_x[1], right_x[0], left_x[0], own_x[2], right_x[1], left_x[1], far_x[0]]
    acc = project(chunks, tokens, other_tokens, [own, a1, r0, l0, a2, r1, l1, far0], None)
    last = [tokens_at(array, (far_x[2], far_x[3])) for array in (tokens, other_tokens)]

    sent_z, sent_r, sent_l, last = tied((b1, r3, l3, last), a3, r2, l2, acc)
    b2, f3, g3 = along_z(sent_z), to_right(sent_r[:half]), to_left(sent_l[half:])
    chunks = [own_x[3], right_x[2], left_x[2], far_x[1], right_x[3], left_x[3]]
    acc = project(chunks, tokens, other_tokens, [a3, r2, l2, b1, r3, l3], acc)
    b2, f3, g3, acc = step((b2, f3, g3, acc))

    shape = (group, DH + TAIL, DH)
    outs = [((2, 2, rows, width), BF16), (shape, F32), (shape, BF16), (shape, F32)]
    kv, chip, sent, first = small_kernel(close_body, outs, place, *last, b2, f3, g3, acc, fades)
    backs = [lax.ppermute(sent, "zl", [(i, (i + j) % 4) for i in range(4)]) for j in (1, 2, 3)]
    outs = [((2, rows, width), BF16), ((2, rows, width), F32)]
    q, intra = small_kernel(functools.partial(intra_body, DH**-0.5), outs, place, *last, b2, f3, acc, kv, fades)
    backs, intra = step((backs, intra))
    before, row = small_kernel(row_body, [(shape, F32), (shape, BF16)], z.reshape(1), chip, *backs)
    backs = [lax.ppermute(row, "x", [(i, i + j) for i in range(4 - j)]) for j in (1, 2, 3)]
    (state,) = small_kernel(incoming_body, [((2, group, 3 * DH, DH), BF16)], place, before, first, *backs)

    attended, squares = by_place(inter_body, [(2, rows, width), (2, 8, rows)], 10**9, q, fades, intra, state)
    squares = squares[:, 0, :]
    got = lax.ppermute(attended[1], "core", SWAP)
    squares = squares + sum(lax.ppermute(squares, "y", [(i, (i + j) % 4) for i in range(4)]) for j in (1, 2, 3))
    summed = squares[0] + lax.ppermute(squares[0], "zh", SWAP) + lax.ppermute(squares[1], "core", SWAP)
    summed = summed + lax.ppermute(squares[1], ("core", "zh"), [(i, 3 - i) for i in range(4)])
    scale = lax.rsqrt(summed / (HEAD_COUNT * DH) + 1e-6)[:, None]
    mine = attended[0]
    whole = jnp.where(core == 0, jnp.concatenate([mine, got], 1), jnp.concatenate([got, mine], 1))
    return (whole * scale * gain[None, :]).astype(BF16)


def solution(mesh):
    fine = Mesh(mesh.devices.reshape(4, 4, 2, 4, 2), ("x", "zl", "core", "y", "zh"))
    seq, head = ("x", "zl", "core"), ("y", "zh")
    return jax.shard_map(
        on_device,
        mesh=fine,
        in_specs=(P(seq, None), P(None, seq, head), P(head, seq), P(head)),
        out_specs=P(seq, head),
        check_vma=False,
    )
```

```python
import functools

import jax
import jax.numpy as jnp
from jax import lax
from jax.experimental import pallas as pl
from jax.experimental.pallas import tpu as pltpu
from jax.sharding import Mesh, PartitionSpec as P

HEAD_COUNT = 32
DH = 128
TAIL = 16
F32, BF16 = jnp.float32, jnp.bfloat16
NEXT = [(i, (i + 1) % 4) for i in range(4)]
LAST = [(i, (i - 1) % 4) for i in range(4)]
SWAP = [(0, 1), (1, 0)]
VMEM_LIMIT = 20 * 1024 * 1024
PROJECT_LIMIT = 54 * 1024 * 1024


ACROSS = (((1,), (1,)), ((), ()))


def tied(value, *others):
    return lax.optimization_barrier((value, others))[0]


def project_body(groups, chunks, has_acc, index_ref, *refs):
    mine, theirs, weights = refs[:chunks], refs[chunks : 2 * chunks], refs[2 * chunks : 3 * chunks]
    accs, outs = refs[3 * chunks : 3 * chunks + len(groups)], refs[-len(groups) :]
    tile, depth = mine[0].shape
    rows = jnp.concatenate(
        [jnp.concatenate([ref[...] for ref in mine], axis=1), jnp.concatenate([ref[...] for ref in theirs], axis=1)], axis=0
    )
    for g, members in enumerate(groups):
        for n, c in enumerate(members):
            w = jnp.concatenate([ref[c * depth : (c + 1) * depth, :] for ref in weights], axis=0)
            total = jnp.dot(rows, w, preferred_element_type=F32)
            for place in range(2):
                part = total[place * tile : (place + 1) * tile]
                outs[g][place, n] = part + accs[g][place, n] if has_acc else part


def project(index, mine, theirs, weights, accs):
    groups = ((0,), (1, 2))
    rows, width = mine.shape[0], weights[0].shape[1]
    depth = weights[0].shape[0] // 3
    tile, chunks = rows // 4, len(index)
    token_specs = [pl.BlockSpec((tile, depth), functools.partial(lambda n, i, ref: (i, ref[n]), n)) for n in range(chunks)]
    weight_specs = [pl.BlockSpec(part.shape, lambda i, ref: (0, 0)) for part in weights]
    out_specs = [pl.BlockSpec((2, len(g), tile, width), lambda i, ref: (0, 0, i, 0)) for g in groups]
    return pl.pallas_call(
        functools.partial(project_body, groups, chunks, accs is not None),
        out_shape=[jax.ShapeDtypeStruct((2, len(g), rows, width), F32) for g in groups],
        grid_spec=pltpu.PrefetchScalarGridSpec(
            num_scalar_prefetch=1,
            grid=(4,),
            in_specs=token_specs * 2 + weight_specs + (out_specs if accs else []),
            out_specs=out_specs,
        ),
        compiler_params=pltpu.CompilerParams(vmem_limit_bytes=PROJECT_LIMIT),
        cost_estimate=pl.CostEstimate(
            flops=12 * rows * depth * chunks * width, bytes_accessed=4 * rows * depth * chunks, transcendentals=0
        ),
    )(jnp.stack(index), *([mine] * chunks), *([theirs] * chunks), *weights, *(accs or []))


def join(earlier, later):
    return jnp.exp(later[1])[:, None, :] * earlier[0] + later[0], earlier[1] + later[1]


def split(value, count):
    parts = []
    for _ in range(count):
        parts.append(value.astype(BF16).astype(F32))
        value = value - parts[-1]
    return parts


def unpack(ref, mask=None):
    state, total = ref[:, :DH, :].astype(F32), jnp.sum(ref[:, DH:, :].astype(F32), axis=1)
    if mask is not None:
        state, total = state * mask, total * mask
    return state, total


def pack(ref, value):
    ref[:, :DH, :] = value[0].astype(ref.dtype)
    row = lax.broadcasted_iota(jnp.int32, (ref.shape[0], TAIL, DH), 1)
    tail = jnp.zeros(row.shape, F32)
    for n, part in enumerate(split(value[1], 3)):
        tail = jnp.where(row == n, part[:, None, :], tail)
    ref[:, DH:, :] = tail.astype(ref.dtype)


def close_body(place_ref, mine_ref, theirs_ref, b_ref, f_ref, g_ref, acc_ref, decay_ref, kv_ref, chip_ref, sent_ref, first_ref):
    group, rows, depth = chip_ref.shape[0], mine_ref.shape[0], b_ref.shape[0] // 3
    half = f_ref.shape[0]
    second_mine = place_ref[0].astype(F32)
    k_weights = jnp.concatenate([b_ref[depth : 2 * depth, :], f_ref[depth:, :], g_ref[: 2 * depth - half, :]], axis=0)
    v_weights = jnp.concatenate([b_ref[2 * depth :, :], g_ref[2 * depth - half :, :]], axis=0)
    states, totals = [], []
    for place, ref in enumerate((mine_ref, theirs_ref)):
        k = (acc_ref[place, 0] + jnp.dot(ref[...], k_weights, preferred_element_type=F32)).astype(BF16)
        v = (acc_ref[place, 1] + jnp.dot(ref[...], v_weights, preferred_element_type=F32)).astype(BF16)
        kv_ref[place, 0] = k
        kv_ref[place, 1] = v
        total = decay_ref[place, :, rows - 1 :]
        tail = jnp.transpose(jnp.exp(total - decay_ref[place]))
        local = []
        for h in range(group):
            cut = slice(h * DH, (h + 1) * DH)
            keys = (k[:, cut].astype(F32) * tail[:, h : h + 1]).astype(BF16)
            local.append(lax.dot_general(keys, v[:, cut], (((0,), (0,)), ((), ())), preferred_element_type=F32))
        states.append(jnp.stack(local))
        totals.append(jnp.broadcast_to(total[:group], (group, DH)))
    first = [jnp.where(second_mine > 0, v[1], v[0]) for v in (states, totals)]
    second = [jnp.where(second_mine > 0, v[0], v[1]) for v in (states, totals)]
    pack(first_ref, first)
    both = join(first, second)
    pack(chip_ref, both)
    pack(sent_ref, both)


def row_body(z_ref, own_ref, back1, back2, back3, before_ref, row_ref):
    z = z_ref[0]
    backs = [back1, back2, back3]
    before = [unpack(ref, (j + 1 <= z).astype(F32)) for j, ref in enumerate(backs)]
    after = [unpack(ref, (j + 1 > z).astype(F32)) for j, ref in enumerate(backs)]
    prefix = join(join(before[2], before[1]), before[0])
    suffix = join(join(after[2], after[1]), after[0])
    pack(before_ref, prefix)
    pack(row_ref, join(join(prefix, unpack(own_ref)), suffix))


def incoming_body(place_ref, before_ref, first_ref, back1, back2, back3, out_ref):
    rows = join(join(unpack(back3), unpack(back2)), unpack(back1))
    state = join(rows, unpack(before_ref))[0]
    first = unpack(first_ref)
    later = jnp.exp(first[1])[:, None, :] * state + first[0]
    mine_second = place_ref[0].astype(F32)
    for place, value in enumerate(
        (jnp.where(mine_second > 0, later, state), jnp.where(mine_second > 0, state, later))
    ):
        for n, part in enumerate(split(value, 3)):
            out_ref[place, :, n * DH : (n + 1) * DH, :] = part.astype(BF16)


def small_kernel(body, outs, scalar, *args):
    return pl.pallas_call(
        body,
        out_shape=[jax.ShapeDtypeStruct(*out) for out in outs],
        in_specs=[pl.BlockSpec(memory_space=pltpu.SMEM)] + [pl.BlockSpec(memory_space=pltpu.VMEM)] * len(args),
        out_specs=[pl.BlockSpec(memory_space=pltpu.VMEM)] * len(outs),
        compiler_params=pltpu.CompilerParams(vmem_limit_bytes=VMEM_LIMIT),
    )(scalar, *args)


def intra_body(scale, place_ref, mine_ref, theirs_ref, b_ref, f_ref, acc_ref, kv_ref, decay_ref, q_ref, out_ref):
    rows, width, depth = mine_ref.shape[0], b_ref.shape[1], b_ref.shape[0] // 3
    i, j = (lax.broadcasted_iota(jnp.int32, (DH, DH), axis) for axis in range(2))
    weights = jnp.concatenate([b_ref[:depth, :], f_ref[:depth, :]], axis=0)
    for place, ref in enumerate((mine_ref, theirs_ref)):
        whole = (acc_ref[place, 0] + jnp.dot(ref[...], weights, preferred_element_type=F32)).astype(BF16)
        q_ref[place] = whole
        columns = jnp.transpose(decay_ref[place])
        for start in range(0, rows, DH):
            stop = start + DH
            for h in range(width // DH):
                cut = slice(h * DH, (h + 1) * DH)
                q = whole[start:stop, cut]
                column, row = columns[start:stop, h : h + 1], decay_ref[place, h : h + 1, :stop]
                raw = lax.dot_general(q, kv_ref[place, 0, :stop, cut], ACROSS, preferred_element_type=F32) * scale
                gap = jnp.where(i >= j, column - row[:, start:], -1e30)
                scores = (raw[:, start:] * jnp.exp(gap)).astype(BF16)
                if start:
                    border = row[:, start - 1 : start]
                    faded = raw[:, :start] * jnp.exp(column - border) * jnp.exp(border - row[:, :start])
                    scores = jnp.concatenate([faded.astype(BF16), scores], axis=1)
                out_ref[place, start:stop, cut] = jnp.dot(
                    scores, kv_ref[place, 1, :stop, cut], preferred_element_type=F32
                )


def inter_body(scale, q_ref, decay_ref, intra_ref, state_ref, out_ref, square_ref):
    rows, width = q_ref.shape[1:]
    squares = jnp.zeros((8, rows), F32)
    grown = jnp.transpose(jnp.exp(decay_ref[0]) * scale)
    for h in range(width // DH):
        cut = slice(h * DH, (h + 1) * DH)
        q = q_ref[0, :, cut]
        inter = jnp.dot(jnp.concatenate([q] * 3, axis=1), state_ref[0, h], preferred_element_type=F32)
        attended = intra_ref[0, :, cut] + inter * grown[:, h : h + 1]
        out_ref[0, :, cut] = attended
        for part in split(attended * attended, 2):
            squares += lax.dot_general(jnp.ones((8, DH), BF16), part.astype(BF16), ACROSS, preferred_element_type=F32)
    square_ref[0] = squares


def by_place(body, outs, flops, *args):
    def whole(shape):
        return pl.BlockSpec((1,) + shape[1:], lambda a: (a,) + (0,) * (len(shape) - 1))

    return pl.pallas_call(
        functools.partial(body, DH**-0.5),
        out_shape=[jax.ShapeDtypeStruct(shape, F32) for shape in outs],
        grid=(2,),
        in_specs=[whole(arg.shape) for arg in args],
        out_specs=[whole(shape) for shape in outs],
        compiler_params=pltpu.CompilerParams(vmem_limit_bytes=VMEM_LIMIT),
        cost_estimate=pl.CostEstimate(flops=flops, bytes_accessed=4 * 10**6, transcendentals=10**6),
    )(*args)


def on_device(tokens, w_qkv, log_decay, gain):
    rows = tokens.shape[0]
    width = w_qkv.shape[2] // 2
    group = width // DH
    x, z, core = lax.axis_index("x"), lax.axis_index("zl"), lax.axis_index("core")
    place = core.reshape(1)

    def halves(array, axis):
        size = array.shape[axis] // 2
        mine = lax.dynamic_slice_in_dim(array, core * size, size, axis)
        theirs = lax.dynamic_slice_in_dim(array, (1 - core) * size, size, axis)
        return mine, theirs

    kept, sent = halves(w_qkv, 2)
    got = lax.ppermute(sent, "core", SWAP)
    own = jnp.where(core == 0, jnp.concatenate([kept, got], 1), jnp.concatenate([got, kept], 1))
    kept, sent = halves(log_decay, 0)
    decay = jnp.stack([kept, lax.ppermute(tied(sent, own), "core", SWAP)])
    other_tokens = lax.ppermute(tied(tokens, own), "core", SWAP)

    fades = jnp.pad(jnp.cumsum(decay, axis=2), ((0, 0), (0, 8 - group), (0, 0)))

    columns = [x, (x + 3) % 4, (x + 1) % 4, (x + 2) % 4]
    index = [[(4 * c + (z + 4 - d) % 4).astype(jnp.int32) for d in range(4)] for c in columns]
    own_x, right_x, left_x, far_x = index

    def along_z(part):
        return lax.ppermute(part, "zl", NEXT)

    def to_right(part):
        return lax.ppermute(part, "x", NEXT)

    def to_left(part):
        return lax.ppermute(part, "x", LAST)

    def tokens_at(array, chunks):
        return jnp.concatenate([lax.dynamic_slice_in_dim(array, c * depth, depth, 1) for c in chunks], axis=1)

    step = lax.optimization_barrier
    depth = own.shape[1]
    own = own.reshape(-1, width)
    half = own.shape[0] // 2
    a1, r0, l0 = along_z(own), to_right(own), to_left(own)

    a2, r1, l1, f0, g0 = along_z(a1), to_right(a1), to_left(a1), to_right(r0[:half]), to_left(l0[half:])

    held = tied(a2, a1, r0, l0)
    a3, r2, l2 = along_z(held), to_right(held), to_left(held)

    far0 = jnp.concatenate([f0, g0])
    sent_z, sent_x = tied((far0, a3), a2, r1, l1, f0, g0)
    b1, r3, l3 = along_z(sent_z), to_right(sent_x), to_left(sent_x)
    chunks = [own_x[0], own_x[1], right_x[0], left_x[0], own_x[2], right_x[1], left_x[1], far_x[0]]
    acc = project(chunks, tokens, other_tokens, [own, a1, r0, l0, a2, r1, l1, far0], None)
    last = [tokens_at(array, (far_x[2], far_x[3])) for array in (tokens, other_tokens)]

    sent_z, sent_r, sent_l, last = tied((b1, r3, l3, last), a3, r2, l2, acc, fades)
    b2, f3, g3 = along_z(sent_z), to_right(sent_r[:half]), to_left(sent_l[half:])
    chunks = [own_x[3], right_x[2], left_x[2], far_x[1], right_x[3], left_x[3]]
    q_acc, kv_acc = project(chunks, tokens, other_tokens, [a3, r2, l2, b1, r3, l3], acc)
    b2, f3, g3, q_acc, kv_acc = step((b2, f3, g3, q_acc, kv_acc))

    shape = (group, DH + TAIL, DH)
    outs = [((2, 2, rows, width), BF16), (shape, F32), (shape, BF16), (shape, F32)]
    kv, chip, sent, first = small_kernel(close_body, outs, place, *last, b2, f3, g3, kv_acc, fades)
    backs = [lax.ppermute(sent, "zl", [(i, (i + j) % 4) for i in range(4)]) for j in (1, 2, 3)]
    outs = [((2, rows, width), BF16), ((2, rows, width), F32)]
    q, intra = small_kernel(functools.partial(intra_body, DH**-0.5), outs, place, *last, b2, f3, q_acc, kv, fades)
    backs, intra = step((backs, intra))
    before, row = small_kernel(row_body, [(shape, F32), (shape, BF16)], z.reshape(1), chip, *backs)
    backs = [lax.ppermute(row, "x", [(i, i + j) for i in range(4 - j)]) for j in (1, 2, 3)]
    (state,) = small_kernel(incoming_body, [((2, group, 3 * DH, DH), BF16)], place, before, first, *backs)

    attended, squares = by_place(inter_body, [(2, rows, width), (2, 8, rows)], 10**9, q, fades, intra, state)
    squares = squares[:, 0, :]
    got = lax.ppermute(attended[1], "core", SWAP)
    squares = squares + sum(lax.ppermute(squares, "y", [(i, (i + j) % 4) for i in range(4)]) for j in (1, 2, 3))
    summed = squares[0] + lax.ppermute(squares[0], "zh", SWAP) + lax.ppermute(squares[1], "core", SWAP)
    summed = summed + lax.ppermute(squares[1], ("core", "zh"), [(i, 3 - i) for i in range(4)])
    scale = lax.rsqrt(summed / (HEAD_COUNT * DH) + 1e-6)[:, None]
    mine = attended[0]
    whole = jnp.where(core == 0, jnp.concatenate([mine, got], 1), jnp.concatenate([got, mine], 1))
    return (whole * scale * gain[None, :]).astype(BF16)


def solution(mesh):
    fine = Mesh(mesh.devices.reshape(4, 4, 2, 4, 2), ("x", "zl", "core", "y", "zh"))
    seq, head = ("x", "zl", "core"), ("y", "zh")
    return jax.shard_map(
        on_device,
        mesh=fine,
        in_specs=(P(seq, None), P(None, seq, head), P(head, seq), P(head)),
        out_specs=P(seq, head),
        check_vma=False,
    )
```

```python
import functools

import jax
import jax.numpy as jnp
from jax import lax
from jax.experimental import pallas as pl
from jax.experimental.pallas import tpu as pltpu
from jax.sharding import Mesh, PartitionSpec as P

HEAD_COUNT = 32
DH = 128
TAIL = 16
F32, BF16 = jnp.float32, jnp.bfloat16
NEXT = [(i, (i + 1) % 4) for i in range(4)]
LAST = [(i, (i - 1) % 4) for i in range(4)]
SWAP = [(0, 1), (1, 0)]
VMEM_LIMIT = 20 * 1024 * 1024
PROJECT_LIMIT = 54 * 1024 * 1024


ACROSS = (((1,), (1,)), ((), ()))


def tied(value, *others):
    return lax.optimization_barrier((value, others))[0]


def project_body(groups, chunks, has_acc, index_ref, *refs):
    mine, theirs, weights = refs[:chunks], refs[chunks : 2 * chunks], refs[2 * chunks : 3 * chunks]
    accs, outs = refs[3 * chunks : 3 * chunks + len(groups)], refs[-len(groups) :]
    tile, depth = mine[0].shape
    rows = jnp.concatenate(
        [jnp.concatenate([ref[...] for ref in mine], axis=1), jnp.concatenate([ref[...] for ref in theirs], axis=1)], axis=0
    )
    for g, members in enumerate(groups):
        for n, c in enumerate(members):
            w = jnp.concatenate([ref[c * depth : (c + 1) * depth, :] for ref in weights], axis=0)
            total = jnp.dot(rows, w, preferred_element_type=F32)
            for place in range(2):
                part = total[place * tile : (place + 1) * tile]
                outs[g][place, n] = part + accs[g][place, n] if has_acc else part


def project(index, mine, theirs, weights, accs):
    groups = ((0,), (1, 2))
    rows, width = mine.shape[0], weights[0].shape[1]
    depth = weights[0].shape[0] // 3
    tile, chunks = rows // 4, len(index)
    token_specs = [pl.BlockSpec((tile, depth), functools.partial(lambda n, i, ref: (i, ref[n]), n)) for n in range(chunks)]
    weight_specs = [pl.BlockSpec(part.shape, lambda i, ref: (0, 0)) for part in weights]
    out_specs = [pl.BlockSpec((2, len(g), tile, width), lambda i, ref: (0, 0, i, 0)) for g in groups]
    return pl.pallas_call(
        functools.partial(project_body, groups, chunks, accs is not None),
        out_shape=[jax.ShapeDtypeStruct((2, len(g), rows, width), F32) for g in groups],
        grid_spec=pltpu.PrefetchScalarGridSpec(
            num_scalar_prefetch=1,
            grid=(4,),
            in_specs=token_specs * 2 + weight_specs + (out_specs if accs else []),
            out_specs=out_specs,
        ),
        compiler_params=pltpu.CompilerParams(vmem_limit_bytes=PROJECT_LIMIT),
        cost_estimate=pl.CostEstimate(
            flops=12 * rows * depth * chunks * width, bytes_accessed=4 * rows * depth * chunks, transcendentals=0
        ),
    )(jnp.stack(index), *([mine] * chunks), *([theirs] * chunks), *weights, *(accs or []))


def join(earlier, later):
    return jnp.exp(later[1])[:, None, :] * earlier[0] + later[0], earlier[1] + later[1]


def split(value, count):
    parts = []
    for _ in range(count):
        parts.append(value.astype(BF16).astype(F32))
        value = value - parts[-1]
    return parts


def unpack(ref, mask=None):
    state, total = ref[:, :DH, :].astype(F32), jnp.sum(ref[:, DH:, :].astype(F32), axis=1)
    if mask is not None:
        state, total = state * mask, total * mask
    return state, total


def pack(ref, value):
    ref[:, :DH, :] = value[0].astype(ref.dtype)
    row = lax.broadcasted_iota(jnp.int32, (ref.shape[0], TAIL, DH), 1)
    tail = jnp.zeros(row.shape, F32)
    for n, part in enumerate(split(value[1], 3)):
        tail = jnp.where(row == n, part[:, None, :], tail)
    ref[:, DH:, :] = tail.astype(ref.dtype)


def close_body(place_ref, mine_ref, theirs_ref, b_ref, f_ref, g_ref, acc_ref, decay_ref, kv_ref, chip_ref, sent_ref, first_ref):
    group, rows, depth = chip_ref.shape[0], mine_ref.shape[0], b_ref.shape[0] // 3
    half = f_ref.shape[0]
    second_mine = place_ref[0].astype(F32)
    k_weights = jnp.concatenate([b_ref[depth : 2 * depth, :], f_ref[depth:, :], g_ref[: 2 * depth - half, :]], axis=0)
    v_weights = jnp.concatenate([b_ref[2 * depth :, :], g_ref[2 * depth - half :, :]], axis=0)
    states, totals = [], []
    for place, ref in enumerate((mine_ref, theirs_ref)):
        k = (acc_ref[place, 0] + jnp.dot(ref[...], k_weights, preferred_element_type=F32)).astype(BF16)
        v = (acc_ref[place, 1] + jnp.dot(ref[...], v_weights, preferred_element_type=F32)).astype(BF16)
        kv_ref[place, 0] = k
        kv_ref[place, 1] = v
        total = decay_ref[place, :, rows - 1 :]
        tail = jnp.transpose(jnp.exp(total - decay_ref[place]))
        local = []
        for h in range(group):
            cut = slice(h * DH, (h + 1) * DH)
            keys = (k[:, cut].astype(F32) * tail[:, h : h + 1]).astype(BF16)
            local.append(lax.dot_general(keys, v[:, cut], (((0,), (0,)), ((), ())), preferred_element_type=F32))
        states.append(jnp.stack(local))
        totals.append(jnp.broadcast_to(total[:group], (group, DH)))
    first = [jnp.where(second_mine > 0, v[1], v[0]) for v in (states, totals)]
    second = [jnp.where(second_mine > 0, v[0], v[1]) for v in (states, totals)]
    pack(first_ref, first)
    both = join(first, second)
    pack(chip_ref, both)
    pack(sent_ref, both)


def row_body(z_ref, own_ref, back1, back2, back3, before_ref, row_ref):
    z = z_ref[0]
    backs = [back1, back2, back3]
    before = [unpack(ref, (j + 1 <= z).astype(F32)) for j, ref in enumerate(backs)]
    after = [unpack(ref, (j + 1 > z).astype(F32)) for j, ref in enumerate(backs)]
    prefix = join(join(before[2], before[1]), before[0])
    suffix = join(join(after[2], after[1]), after[0])
    pack(before_ref, prefix)
    pack(row_ref, join(join(prefix, unpack(own_ref)), suffix))


def incoming_body(place_ref, before_ref, first_ref, back1, back2, back3, out_ref):
    rows = join(join(unpack(back3), unpack(back2)), unpack(back1))
    state = join(rows, unpack(before_ref))[0]
    first = unpack(first_ref)
    later = jnp.exp(first[1])[:, None, :] * state + first[0]
    mine_second = place_ref[0].astype(F32)
    for place, value in enumerate(
        (jnp.where(mine_second > 0, later, state), jnp.where(mine_second > 0, state, later))
    ):
        for n, part in enumerate(split(value, 3)):
            out_ref[place, :, n * DH : (n + 1) * DH, :] = part.astype(BF16)


def small_kernel(body, outs, scalar, *args):
    return pl.pallas_call(
        body,
        out_shape=[jax.ShapeDtypeStruct(*out) for out in outs],
        in_specs=[pl.BlockSpec(memory_space=pltpu.SMEM)] + [pl.BlockSpec(memory_space=pltpu.VMEM)] * len(args),
        out_specs=[pl.BlockSpec(memory_space=pltpu.VMEM)] * len(outs),
        compiler_params=pltpu.CompilerParams(vmem_limit_bytes=VMEM_LIMIT),
    )(scalar, *args)


def intra_body(scale, place_ref, mine_ref, theirs_ref, b_ref, f_ref, acc_ref, kv_ref, decay_ref, q_ref, out_ref):
    rows, width, depth = mine_ref.shape[0], b_ref.shape[1], b_ref.shape[0] // 3
    i, j = (lax.broadcasted_iota(jnp.int32, (DH, DH), axis) for axis in range(2))
    weights = jnp.concatenate([b_ref[:depth, :], f_ref[:depth, :]], axis=0)
    for place, ref in enumerate((mine_ref, theirs_ref)):
        whole = (acc_ref[place, 0] + jnp.dot(ref[...], weights, preferred_element_type=F32)).astype(BF16)
        q_ref[place] = whole
        columns = jnp.transpose(decay_ref[place])
        for start in range(0, rows, DH):
            stop = start + DH
            for h in range(width // DH):
                cut = slice(h * DH, (h + 1) * DH)
                q = whole[start:stop, cut]
                column, row = columns[start:stop, h : h + 1], decay_ref[place, h : h + 1, :stop]
                raw = lax.dot_general(q, kv_ref[place, 0, :stop, cut], ACROSS, preferred_element_type=F32) * scale
                gap = jnp.where(i >= j, column - row[:, start:], -1e30)
                scores = (raw[:, start:] * jnp.exp(gap)).astype(BF16)
                if start:
                    border = row[:, start - 1 : start]
                    faded = raw[:, :start] * jnp.exp(column - border) * jnp.exp(border - row[:, :start])
                    scores = jnp.concatenate([faded.astype(BF16), scores], axis=1)
                out_ref[place, start:stop, cut] = jnp.dot(
                    scores, kv_ref[place, 1, :stop, cut], preferred_element_type=F32
                )


def inter_body(scale, q_ref, decay_ref, intra_ref, state_ref, out_ref, square_ref):
    rows, width = q_ref.shape[1:]
    squares = jnp.zeros((8, rows), F32)
    grown = jnp.transpose(jnp.exp(decay_ref[0]) * scale)
    for h in range(width // DH):
        cut = slice(h * DH, (h + 1) * DH)
        q = q_ref[0, :, cut]
        inter = jnp.dot(jnp.concatenate([q] * 3, axis=1), state_ref[0, h], preferred_element_type=F32)
        attended = intra_ref[0, :, cut] + inter * grown[:, h : h + 1]
        out_ref[0, :, cut] = attended
        for part in split(attended * attended, 2):
            squares += lax.dot_general(jnp.ones((8, DH), BF16), part.astype(BF16), ACROSS, preferred_element_type=F32)
    square_ref[0] = squares


def by_place(body, outs, flops, *args):
    def whole(shape):
        return pl.BlockSpec((1,) + shape[1:], lambda a: (a,) + (0,) * (len(shape) - 1))

    return pl.pallas_call(
        functools.partial(body, DH**-0.5),
        out_shape=[jax.ShapeDtypeStruct(shape, F32) for shape in outs],
        grid=(2,),
        in_specs=[whole(arg.shape) for arg in args],
        out_specs=[whole(shape) for shape in outs],
        compiler_params=pltpu.CompilerParams(vmem_limit_bytes=VMEM_LIMIT),
        cost_estimate=pl.CostEstimate(flops=flops, bytes_accessed=4 * 10**6, transcendentals=10**6),
    )(*args)


def on_device(tokens, w_qkv, log_decay, gain):
    rows = tokens.shape[0]
    width = w_qkv.shape[2] // 2
    group = width // DH
    x, z, core = lax.axis_index("x"), lax.axis_index("zl"), lax.axis_index("core")
    place = core.reshape(1)

    def halves(array, axis):
        size = array.shape[axis] // 2
        mine = lax.dynamic_slice_in_dim(array, core * size, size, axis)
        theirs = lax.dynamic_slice_in_dim(array, (1 - core) * size, size, axis)
        return mine, theirs

    kept, sent = halves(w_qkv, 2)
    got = lax.ppermute(sent, "core", SWAP)
    own = jnp.where(core == 0, jnp.concatenate([kept, got], 1), jnp.concatenate([got, kept], 1))
    kept, sent = halves(log_decay, 0)
    decay = jnp.stack([kept, lax.ppermute(tied(sent, own), "core", SWAP)])
    other_tokens = lax.ppermute(tied(tokens, own), "core", SWAP)

    fades = jnp.pad(jnp.cumsum(decay, axis=2), ((0, 0), (0, 8 - group), (0, 0)))

    columns = [x, (x + 3) % 4, (x + 1) % 4, (x + 2) % 4]
    index = [[(4 * c + (z + 4 - d) % 4).astype(jnp.int32) for d in range(4)] for c in columns]
    own_x, right_x, left_x, far_x = index

    def along_z(part):
        return lax.ppermute(part, "zl", NEXT)

    def to_right(part):
        return lax.ppermute(part, "x", NEXT)

    def to_left(part):
        return lax.ppermute(part, "x", LAST)

    def tokens_at(array, chunks):
        return jnp.concatenate([lax.dynamic_slice_in_dim(array, c * depth, depth, 1) for c in chunks], axis=1)

    step = lax.optimization_barrier
    depth = own.shape[1]
    own = own.reshape(-1, width)
    half = own.shape[0] // 2
    a1, r0, l0 = along_z(own), to_right(own), to_left(own)

    a2, r1, l1, f0, g0 = along_z(a1), to_right(a1), to_left(a1), to_right(r0[:half]), to_left(l0[half:])

    held = tied(a2, a1, r0, l0)
    a3, r2, l2 = along_z(held), to_right(held), to_left(held)

    far0 = jnp.concatenate([f0, g0])
    sent_z, sent_x = tied((far0, a3), a2, r1, l1, f0, g0)
    b1, r3, l3 = along_z(sent_z), to_right(sent_x), to_left(sent_x)
    chunks = [own_x[0], own_x[1], right_x[0], left_x[0], own_x[2], right_x[1], left_x[1], far_x[0]]
    acc = project(chunks, tokens, other_tokens, [own, a1, r0, l0, a2, r1, l1, far0], None)
    last = [tokens_at(array, (far_x[2], far_x[3])) for array in (tokens, other_tokens)]

    sent_z, sent_r, sent_l, last = tied((b1, r3, l3, last), a3, r2, l2, acc, fades)
    b2, f3, g3 = along_z(sent_z), to_right(sent_r[:half]), to_left(sent_l[half:])
    chunks = [own_x[3], right_x[2], left_x[2], far_x[1], right_x[3], left_x[3]]
    q_acc, kv_acc = project(chunks, tokens, other_tokens, [a3, r2, l2, b1, r3, l3], acc)
    b2, f3, g3, q_acc, kv_acc = step((b2, f3, g3, q_acc, kv_acc))

    shape = (group, DH + TAIL, DH)
    outs = [((2, 2, rows, width), BF16), (shape, F32), (shape, BF16), (shape, F32)]
    kv, chip, sent, first = small_kernel(close_body, outs, place, *last, b2, f3, g3, kv_acc, fades)
    backs = [lax.ppermute(sent, "zl", [(i, (i + j) % 4) for i in range(4)]) for j in (1, 2, 3)]
    outs = [((2, rows, width), BF16), ((2, rows, width), F32)]
    q, intra = small_kernel(functools.partial(intra_body, DH**-0.5), outs, place, *last, b2, f3, q_acc, kv, fades)
    backs, intra = step((backs, intra))
    before, row = small_kernel(row_body, [(shape, F32), (shape, BF16)], z.reshape(1), chip, *backs)
    backs = [lax.ppermute(row, "x", [(i, i + j) for i in range(4 - j)]) for j in (1, 2, 3)]
    (state,) = small_kernel(incoming_body, [((2, group, 3 * DH, DH), BF16)], place, before, first, *backs)

    attended, squares = by_place(inter_body, [(2, rows, width), (2, 8, rows)], 10**9, q, fades, intra, state)
    squares = squares[:, 0, :]
    summed = squares[0] + lax.ppermute(squares[1], "core", SWAP)
    got = lax.ppermute(tied(attended[1], summed), "core", SWAP)
    summed = summed + sum(lax.ppermute(summed, "y", [(i, (i + j) % 4) for i in range(4)]) for j in (1, 2, 3))
    summed = summed + lax.ppermute(summed, "zh", SWAP)
    scale = lax.rsqrt(summed / (HEAD_COUNT * DH) + 1e-6)[:, None]
    mine = attended[0]
    whole = jnp.where(core == 0, jnp.concatenate([mine, got], 1), jnp.concatenate([got, mine], 1))
    return (whole * scale * gain[None, :]).astype(BF16)


def solution(mesh):
    fine = Mesh(mesh.devices.reshape(4, 4, 2, 4, 2), ("x", "zl", "core", "y", "zh"))
    seq, head = ("x", "zl", "core"), ("y", "zh")
    return jax.shard_map(
        on_device,
        mesh=fine,
        in_specs=(P(seq, None), P(None, seq, head), P(head, seq), P(head)),
        out_specs=P(seq, head),
        check_vma=False,
    )
```

```python
import functools

import jax
import jax.numpy as jnp
from jax import lax
from jax.experimental import pallas as pl
from jax.experimental.pallas import tpu as pltpu
from jax.sharding import Mesh, PartitionSpec as P

HEAD_COUNT = 32
DH = 128
TAIL = 16
F32, BF16 = jnp.float32, jnp.bfloat16
NEXT = [(i, (i + 1) % 4) for i in range(4)]
LAST = [(i, (i - 1) % 4) for i in range(4)]
SWAP = [(0, 1), (1, 0)]
VMEM_LIMIT = 20 * 1024 * 1024
PROJECT_LIMIT = 54 * 1024 * 1024


ACROSS = (((1,), (1,)), ((), ()))


def tied(value, *others):
    return lax.optimization_barrier((value, others))[0]


def project_body(groups, chunks, has_acc, index_ref, *refs):
    mine, theirs, weights = refs[:chunks], refs[chunks : 2 * chunks], refs[2 * chunks : 3 * chunks]
    accs, outs = refs[3 * chunks : 3 * chunks + len(groups)], refs[-len(groups) :]
    tile, depth = mine[0].shape
    rows = jnp.concatenate(
        [jnp.concatenate([ref[...] for ref in mine], axis=1), jnp.concatenate([ref[...] for ref in theirs], axis=1)], axis=0
    )
    for g, members in enumerate(groups):
        for n, c in enumerate(members):
            w = jnp.concatenate([ref[c * depth : (c + 1) * depth, :] for ref in weights], axis=0)
            total = jnp.dot(rows, w, preferred_element_type=F32)
            for place in range(2):
                part = total[place * tile : (place + 1) * tile]
                outs[g][place, n] = part + accs[g][place, n] if has_acc else part


def project(index, mine, theirs, weights, accs):
    groups = ((0,), (1, 2))
    rows, width = mine.shape[0], weights[0].shape[1]
    depth = weights[0].shape[0] // 3
    tile, chunks = rows // 4, len(index)
    token_specs = [pl.BlockSpec((tile, depth), functools.partial(lambda n, i, ref: (i, ref[n]), n)) for n in range(chunks)]
    weight_specs = [pl.BlockSpec(part.shape, lambda i, ref: (0, 0)) for part in weights]
    out_specs = [pl.BlockSpec((2, len(g), tile, width), lambda i, ref: (0, 0, i, 0)) for g in groups]
    return pl.pallas_call(
        functools.partial(project_body, groups, chunks, accs is not None),
        out_shape=[jax.ShapeDtypeStruct((2, len(g), rows, width), F32) for g in groups],
        grid_spec=pltpu.PrefetchScalarGridSpec(
            num_scalar_prefetch=1,
            grid=(4,),
            in_specs=token_specs * 2 + weight_specs + (out_specs if accs else []),
            out_specs=out_specs,
        ),
        compiler_params=pltpu.CompilerParams(vmem_limit_bytes=PROJECT_LIMIT),
        cost_estimate=pl.CostEstimate(
            flops=12 * rows * depth * chunks * width, bytes_accessed=4 * rows * depth * chunks, transcendentals=0
        ),
    )(jnp.stack(index), *([mine] * chunks), *([theirs] * chunks), *weights, *(accs or []))


def join(earlier, later):
    return jnp.exp(later[1])[:, None, :] * earlier[0] + later[0], earlier[1] + later[1]


def split(value, count):
    parts = []
    for _ in range(count):
        parts.append(value.astype(BF16).astype(F32))
        value = value - parts[-1]
    return parts


def unpack(ref, mask=None):
    state, total = ref[:, :DH, :].astype(F32), jnp.sum(ref[:, DH:, :].astype(F32), axis=1)
    if mask is not None:
        state, total = state * mask, total * mask
    return state, total


def pack(ref, value):
    ref[:, :DH, :] = value[0].astype(ref.dtype)
    row = lax.broadcasted_iota(jnp.int32, (ref.shape[0], TAIL, DH), 1)
    tail = jnp.zeros(row.shape, F32)
    for n, part in enumerate(split(value[1], 3)):
        tail = jnp.where(row == n, part[:, None, :], tail)
    ref[:, DH:, :] = tail.astype(ref.dtype)


def close_body(place_ref, mine_ref, theirs_ref, b_ref, f_ref, g_ref, acc_ref, decay_ref, kv_ref, chip_ref, sent_ref, first_ref):
    group, rows, depth = chip_ref.shape[0], mine_ref.shape[0], b_ref.shape[0] // 3
    half = f_ref.shape[0]
    second_mine = place_ref[0].astype(F32)
    k_weights = jnp.concatenate([b_ref[depth : 2 * depth, :], f_ref[depth:, :], g_ref[: 2 * depth - half, :]], axis=0)
    v_weights = jnp.concatenate([b_ref[2 * depth :, :], g_ref[2 * depth - half :, :]], axis=0)
    states, totals = [], []
    for place, ref in enumerate((mine_ref, theirs_ref)):
        k = (acc_ref[place, 0] + jnp.dot(ref[...], k_weights, preferred_element_type=F32)).astype(BF16)
        v = (acc_ref[place, 1] + jnp.dot(ref[...], v_weights, preferred_element_type=F32)).astype(BF16)
        kv_ref[place, 0] = k
        kv_ref[place, 1] = v
        total = decay_ref[place, :, rows - 1 :]
        tail = jnp.transpose(jnp.exp(total - decay_ref[place]))
        local = []
        for h in range(group):
            cut = slice(h * DH, (h + 1) * DH)
            keys = (k[:, cut].astype(F32) * tail[:, h : h + 1]).astype(BF16)
            local.append(lax.dot_general(keys, v[:, cut], (((0,), (0,)), ((), ())), preferred_element_type=F32))
        states.append(jnp.stack(local))
        totals.append(jnp.broadcast_to(total[:group], (group, DH)))
    first = [jnp.where(second_mine > 0, v[1], v[0]) for v in (states, totals)]
    second = [jnp.where(second_mine > 0, v[0], v[1]) for v in (states, totals)]
    pack(first_ref, first)
    both = join(first, second)
    pack(chip_ref, both)
    pack(sent_ref, both)


def row_body(z_ref, own_ref, back1, back2, back3, before_ref, row_ref):
    z = z_ref[0]
    backs = [back1, back2, back3]
    before = [unpack(ref, (j + 1 <= z).astype(F32)) for j, ref in enumerate(backs)]
    after = [unpack(ref, (j + 1 > z).astype(F32)) for j, ref in enumerate(backs)]
    prefix = join(join(before[2], before[1]), before[0])
    suffix = join(join(after[2], after[1]), after[0])
    pack(before_ref, prefix)
    pack(row_ref, join(join(prefix, unpack(own_ref)), suffix))


def incoming_body(place_ref, before_ref, first_ref, back1, back2, back3, out_ref):
    x = place_ref[1]
    back = [unpack(ref, (j + 1 <= x).astype(F32)) for j, ref in enumerate((back1, back2, back3))]
    rows = join(join(back[2], back[1]), back[0])
    state = join(rows, unpack(before_ref))[0]
    first = unpack(first_ref)
    later = jnp.exp(first[1])[:, None, :] * state + first[0]
    mine_second = place_ref[0].astype(F32)
    for place, value in enumerate(
        (jnp.where(mine_second > 0, later, state), jnp.where(mine_second > 0, state, later))
    ):
        for n, part in enumerate(split(value, 3)):
            out_ref[place, :, n * DH : (n + 1) * DH, :] = part.astype(BF16)


def small_kernel(body, outs, scalar, *args):
    return pl.pallas_call(
        body,
        out_shape=[jax.ShapeDtypeStruct(*out) for out in outs],
        in_specs=[pl.BlockSpec(memory_space=pltpu.SMEM)] + [pl.BlockSpec(memory_space=pltpu.VMEM)] * len(args),
        out_specs=[pl.BlockSpec(memory_space=pltpu.VMEM)] * len(outs),
        compiler_params=pltpu.CompilerParams(vmem_limit_bytes=VMEM_LIMIT),
    )(scalar, *args)


def intra_body(scale, place_ref, mine_ref, theirs_ref, b_ref, f_ref, acc_ref, kv_ref, decay_ref, q_ref, out_ref):
    rows, width, depth = mine_ref.shape[0], b_ref.shape[1], b_ref.shape[0] // 3
    i, j = (lax.broadcasted_iota(jnp.int32, (DH, DH), axis) for axis in range(2))
    weights = jnp.concatenate([b_ref[:depth, :], f_ref[:depth, :]], axis=0)
    for place, ref in enumerate((mine_ref, theirs_ref)):
        whole = (acc_ref[place, 0] + jnp.dot(ref[...], weights, preferred_element_type=F32)).astype(BF16)
        q_ref[place] = whole
        columns = jnp.transpose(decay_ref[place])
        for start in range(0, rows, DH):
            stop = start + DH
            for h in range(width // DH):
                cut = slice(h * DH, (h + 1) * DH)
                q = whole[start:stop, cut]
                column, row = columns[start:stop, h : h + 1], decay_ref[place, h : h + 1, :stop]
                raw = lax.dot_general(q, kv_ref[place, 0, :stop, cut], ACROSS, preferred_element_type=F32) * scale
                gap = jnp.where(i >= j, column - row[:, start:], -1e30)
                scores = (raw[:, start:] * jnp.exp(gap)).astype(BF16)
                if start:
                    border = row[:, start - 1 : start]
                    faded = raw[:, :start] * jnp.exp(column - border) * jnp.exp(border - row[:, :start])
                    scores = jnp.concatenate([faded.astype(BF16), scores], axis=1)
                out_ref[place, start:stop, cut] = jnp.dot(
                    scores, kv_ref[place, 1, :stop, cut], preferred_element_type=F32
                )


def inter_body(scale, q_ref, decay_ref, intra_ref, state_ref, out_ref, square_ref):
    rows, width = q_ref.shape[1:]
    squares = jnp.zeros((8, rows), F32)
    grown = jnp.transpose(jnp.exp(decay_ref[0]) * scale)
    for h in range(width // DH):
        cut = slice(h * DH, (h + 1) * DH)
        q = q_ref[0, :, cut]
        inter = jnp.dot(jnp.concatenate([q] * 3, axis=1), state_ref[0, h], preferred_element_type=F32)
        attended = intra_ref[0, :, cut] + inter * grown[:, h : h + 1]
        out_ref[0, :, cut] = attended
        for part in split(attended * attended, 2):
            squares += lax.dot_general(jnp.ones((8, DH), BF16), part.astype(BF16), ACROSS, preferred_element_type=F32)
    square_ref[0] = squares


def by_place(body, outs, flops, *args):
    def whole(shape):
        return pl.BlockSpec((1,) + shape[1:], lambda a: (a,) + (0,) * (len(shape) - 1))

    return pl.pallas_call(
        functools.partial(body, DH**-0.5),
        out_shape=[jax.ShapeDtypeStruct(shape, F32) for shape in outs],
        grid=(2,),
        in_specs=[whole(arg.shape) for arg in args],
        out_specs=[whole(shape) for shape in outs],
        compiler_params=pltpu.CompilerParams(vmem_limit_bytes=VMEM_LIMIT),
        cost_estimate=pl.CostEstimate(flops=flops, bytes_accessed=4 * 10**6, transcendentals=10**6),
    )(*args)


def on_device(tokens, w_qkv, log_decay, gain):
    rows = tokens.shape[0]
    width = w_qkv.shape[2] // 2
    group = width // DH
    x, z, core = lax.axis_index("x"), lax.axis_index("zl"), lax.axis_index("core")
    place = core.reshape(1)

    def halves(array, axis):
        size = array.shape[axis] // 2
        mine = lax.dynamic_slice_in_dim(array, core * size, size, axis)
        theirs = lax.dynamic_slice_in_dim(array, (1 - core) * size, size, axis)
        return mine, theirs

    kept, sent = halves(w_qkv, 2)
    got = lax.ppermute(sent, "core", SWAP)
    own = jnp.where(core == 0, jnp.concatenate([kept, got], 1), jnp.concatenate([got, kept], 1))
    kept, sent = halves(log_decay, 0)
    decay = jnp.stack([kept, lax.ppermute(tied(sent, own), "core", SWAP)])
    other_tokens = lax.ppermute(tied(tokens, own), "core", SWAP)

    fades = jnp.pad(jnp.cumsum(decay, axis=2), ((0, 0), (0, 8 - group), (0, 0)))

    columns = [x, (x + 3) % 4, (x + 1) % 4, (x + 2) % 4]
    index = [[(4 * c + (z + 4 - d) % 4).astype(jnp.int32) for d in range(4)] for c in columns]
    own_x, right_x, left_x, far_x = index

    def along_z(part):
        return lax.ppermute(part, "zl", NEXT)

    def to_right(part):
        return lax.ppermute(part, "x", NEXT)

    def to_left(part):
        return lax.ppermute(part, "x", LAST)

    def tokens_at(array, chunks):
        return jnp.concatenate([lax.dynamic_slice_in_dim(array, c * depth, depth, 1) for c in chunks], axis=1)

    step = lax.optimization_barrier
    depth = own.shape[1]
    own = own.reshape(-1, width)
    half = own.shape[0] // 2
    a1, r0, l0 = along_z(own), to_right(own), to_left(own)

    a2, r1, l1, f0, g0 = along_z(a1), to_right(a1), to_left(a1), to_right(r0[:half]), to_left(l0[half:])

    held = tied(a2, a1, r0, l0)
    a3, r2, l2 = along_z(held), to_right(held), to_left(held)

    far0 = jnp.concatenate([f0, g0])
    sent_z, sent_x = tied((far0, a3), a2, r1, l1, f0, g0)
    b1, r3, l3 = along_z(sent_z), to_right(sent_x), to_left(sent_x)
    chunks = [own_x[0], own_x[1], right_x[0], left_x[0], own_x[2], right_x[1], left_x[1], far_x[0]]
    acc = project(chunks, tokens, other_tokens, [own, a1, r0, l0, a2, r1, l1, far0], None)
    last = [tokens_at(array, (far_x[2], far_x[3])) for array in (tokens, other_tokens)]

    sent_z, sent_r, sent_l, last = tied((b1, r3, l3, last), a3, r2, l2, acc, fades)
    b2, f3, g3 = along_z(sent_z), to_right(sent_r[:half]), to_left(sent_l[half:])
    chunks = [own_x[3], right_x[2], left_x[2], far_x[1], right_x[3], left_x[3]]
    q_acc, kv_acc = project(chunks, tokens, other_tokens, [a3, r2, l2, b1, r3, l3], acc)
    b2, f3, g3, q_acc, kv_acc = step((b2, f3, g3, q_acc, kv_acc))

    shape = (group, DH + TAIL, DH)
    outs = [((2, 2, rows, width), BF16), (shape, F32), (shape, BF16), (shape, F32)]
    kv, chip, sent, first = small_kernel(close_body, outs, place, *last, b2, f3, g3, kv_acc, fades)
    backs = [lax.ppermute(sent, "zl", [(i, (i + j) % 4) for i in range(4)]) for j in (1, 2, 3)]
    outs = [((2, rows, width), BF16), ((2, rows, width), F32)]
    q, intra = small_kernel(functools.partial(intra_body, DH**-0.5), outs, place, *last, b2, f3, q_acc, kv, fades)
    backs, intra = step((backs, intra))
    before, row = small_kernel(row_body, [(shape, F32), (shape, BF16)], z.reshape(1), chip, *backs)
    backs = [lax.ppermute(row, "x", [(i, (i + j) % 4) for i in range(4)]) for j in (1, 2, 3)]
    (state,) = small_kernel(incoming_body, [((2, group, 3 * DH, DH), BF16)], jnp.stack([core, x]), before, first, *backs)

    attended, squares = by_place(inter_body, [(2, rows, width), (2, 8, rows)], 10**9, q, fades, intra, state)
    squares = squares[:, 0, :]
    summed = squares[0] + lax.ppermute(squares[1], "core", SWAP)
    got = lax.ppermute(tied(attended[1], summed), "core", SWAP)
    summed = summed + sum(lax.ppermute(summed, "y", [(i, (i + j) % 4) for i in range(4)]) for j in (1, 2, 3))
    summed = summed + lax.ppermute(summed, "zh", SWAP)
    scale = lax.rsqrt(summed / (HEAD_COUNT * DH) + 1e-6)[:, None]
    mine = attended[0]
    whole = jnp.where(core == 0, jnp.concatenate([mine, got], 1), jnp.concatenate([got, mine], 1))
    return (whole * scale * gain[None, :]).astype(BF16)


def solution(mesh):
    fine = Mesh(mesh.devices.reshape(4, 4, 2, 4, 2), ("x", "zl", "core", "y", "zh"))
    seq, head = ("x", "zl", "core"), ("y", "zh")
    return jax.shard_map(
        on_device,
        mesh=fine,
        in_specs=(P(seq, None), P(None, seq, head), P(head, seq), P(head)),
        out_specs=P(seq, head),
        check_vma=False,
    )
```

```python
import functools

import jax
import jax.numpy as jnp
from jax import lax
from jax.experimental import pallas as pl
from jax.experimental.pallas import tpu as pltpu
from jax.sharding import Mesh, PartitionSpec as P

HEAD_COUNT = 32
DH = 128
TAIL = 16
F32, BF16 = jnp.float32, jnp.bfloat16
NEXT = [(i, (i + 1) % 4) for i in range(4)]
LAST = [(i, (i - 1) % 4) for i in range(4)]
SWAP = [(0, 1), (1, 0)]
VMEM_LIMIT = 20 * 1024 * 1024
PROJECT_LIMIT = 54 * 1024 * 1024


ACROSS = (((1,), (1,)), ((), ()))


def tied(value, *others):
    return lax.optimization_barrier((value, others))[0]


def project_body(groups, chunks, has_acc, index_ref, *refs):
    mine, theirs, weights = refs[:chunks], refs[chunks : 2 * chunks], refs[2 * chunks : 3 * chunks]
    accs, outs = refs[3 * chunks : 3 * chunks + len(groups)], refs[-len(groups) :]
    tile, depth = mine[0].shape
    rows = jnp.concatenate(
        [jnp.concatenate([ref[...] for ref in mine], axis=1), jnp.concatenate([ref[...] for ref in theirs], axis=1)], axis=0
    )
    for g, members in enumerate(groups):
        for n, c in enumerate(members):
            w = jnp.concatenate([ref[c * depth : (c + 1) * depth, :] for ref in weights], axis=0)
            total = jnp.dot(rows, w, preferred_element_type=F32)
            for place in range(2):
                part = total[place * tile : (place + 1) * tile]
                outs[g][place, n] = part + accs[g][place, n] if has_acc else part


def project(index, mine, theirs, weights, accs):
    groups = ((0,), (1, 2))
    rows, width = mine.shape[0], weights[0].shape[1]
    depth = weights[0].shape[0] // 3
    tile, chunks = rows // 4, len(index)
    token_specs = [pl.BlockSpec((tile, depth), functools.partial(lambda n, i, ref: (i, ref[n]), n)) for n in range(chunks)]
    weight_specs = [pl.BlockSpec(part.shape, lambda i, ref: (0, 0)) for part in weights]
    out_specs = [pl.BlockSpec((2, len(g), tile, width), lambda i, ref: (0, 0, i, 0)) for g in groups]
    return pl.pallas_call(
        functools.partial(project_body, groups, chunks, accs is not None),
        out_shape=[jax.ShapeDtypeStruct((2, len(g), rows, width), F32) for g in groups],
        grid_spec=pltpu.PrefetchScalarGridSpec(
            num_scalar_prefetch=1,
            grid=(4,),
            in_specs=token_specs * 2 + weight_specs + (out_specs if accs else []),
            out_specs=out_specs,
        ),
        compiler_params=pltpu.CompilerParams(vmem_limit_bytes=PROJECT_LIMIT),
        cost_estimate=pl.CostEstimate(
            flops=12 * rows * depth * chunks * width, bytes_accessed=4 * rows * depth * chunks, transcendentals=0
        ),
    )(jnp.stack(index), *([mine] * chunks), *([theirs] * chunks), *weights, *(accs or []))


def join(earlier, later):
    return jnp.exp(later[1])[:, None, :] * earlier[0] + later[0], earlier[1] + later[1]


def split(value, count):
    parts = []
    for _ in range(count):
        parts.append(value.astype(BF16).astype(F32))
        value = value - parts[-1]
    return parts


def unpack(ref, mask=None):
    state, total = ref[:, :DH, :].astype(F32), jnp.sum(ref[:, DH:, :].astype(F32), axis=1)
    if mask is not None:
        state, total = state * mask, total * mask
    return state, total


def pack(ref, value):
    ref[:, :DH, :] = value[0].astype(ref.dtype)
    row = lax.broadcasted_iota(jnp.int32, (ref.shape[0], TAIL, DH), 1)
    tail = jnp.zeros(row.shape, F32)
    for n, part in enumerate(split(value[1], 3)):
        tail = jnp.where(row == n, part[:, None, :], tail)
    ref[:, DH:, :] = tail.astype(ref.dtype)


def close_body(place_ref, mine_ref, theirs_ref, b_ref, f_ref, g_ref, acc_ref, decay_ref, kv_ref, chip_ref, sent_ref, first_ref):
    group, rows, depth = chip_ref.shape[0], mine_ref.shape[0], b_ref.shape[0] // 3
    half = f_ref.shape[0]
    second_mine = place_ref[0].astype(F32)
    k_weights = jnp.concatenate([b_ref[depth : 2 * depth, :], f_ref[depth:, :], g_ref[: 2 * depth - half, :]], axis=0)
    v_weights = jnp.concatenate([b_ref[2 * depth :, :], g_ref[2 * depth - half :, :]], axis=0)
    states, totals = [], []
    for place, ref in enumerate((mine_ref, theirs_ref)):
        k = (acc_ref[place, 0] + jnp.dot(ref[...], k_weights, preferred_element_type=F32)).astype(BF16)
        v = (acc_ref[place, 1] + jnp.dot(ref[...], v_weights, preferred_element_type=F32)).astype(BF16)
        kv_ref[place, 0] = k
        kv_ref[place, 1] = v
        total = decay_ref[place, :, rows - 1 :]
        tail = jnp.transpose(jnp.exp(total - decay_ref[place]))
        local = []
        for h in range(group):
            cut = slice(h * DH, (h + 1) * DH)
            keys = (k[:, cut].astype(F32) * tail[:, h : h + 1]).astype(BF16)
            local.append(lax.dot_general(keys, v[:, cut], (((0,), (0,)), ((), ())), preferred_element_type=F32))
        states.append(jnp.stack(local))
        totals.append(jnp.broadcast_to(total[:group], (group, DH)))
    first = [jnp.where(second_mine > 0, v[1], v[0]) for v in (states, totals)]
    second = [jnp.where(second_mine > 0, v[0], v[1]) for v in (states, totals)]
    pack(first_ref, first)
    both = join(first, second)
    pack(chip_ref, both)
    pack(sent_ref, both)


def row_body(z_ref, own_ref, back1, back2, back3, before_ref, row_ref):
    z = z_ref[0]
    backs = [back1, back2, back3]
    before = [unpack(ref, (j + 1 <= z).astype(F32)) for j, ref in enumerate(backs)]
    after = [unpack(ref, (j + 1 > z).astype(F32)) for j, ref in enumerate(backs)]
    prefix = join(join(before[2], before[1]), before[0])
    suffix = join(join(after[2], after[1]), after[0])
    pack(before_ref, prefix)
    pack(row_ref, join(join(prefix, unpack(own_ref)), suffix))


def incoming_body(place_ref, before_ref, first_ref, back1, back2, back3, out_ref):
    x = place_ref[1]
    back = [unpack(ref, (j + 1 <= x).astype(F32)) for j, ref in enumerate((back1, back2, back3))]
    rows = join(join(back[2], back[1]), back[0])
    state = join(rows, unpack(before_ref))[0]
    first = unpack(first_ref)
    later = jnp.exp(first[1])[:, None, :] * state + first[0]
    mine_second = place_ref[0].astype(F32)
    for place, value in enumerate(
        (jnp.where(mine_second > 0, later, state), jnp.where(mine_second > 0, state, later))
    ):
        for n, part in enumerate(split(value, 3)):
            out_ref[place, :, n * DH : (n + 1) * DH, :] = part.astype(BF16)


def small_kernel(body, outs, scalar, *args):
    return pl.pallas_call(
        body,
        out_shape=[jax.ShapeDtypeStruct(*out) for out in outs],
        in_specs=[pl.BlockSpec(memory_space=pltpu.SMEM)] + [pl.BlockSpec(memory_space=pltpu.VMEM)] * len(args),
        out_specs=[pl.BlockSpec(memory_space=pltpu.VMEM)] * len(outs),
        compiler_params=pltpu.CompilerParams(vmem_limit_bytes=VMEM_LIMIT),
    )(scalar, *args)


def intra_body(scale, place_ref, mine_ref, theirs_ref, b_ref, f_ref, acc_ref, kv_ref, decay_ref, q_ref, out_ref):
    rows, width, depth = mine_ref.shape[0], b_ref.shape[1], b_ref.shape[0] // 3
    i, j = (lax.broadcasted_iota(jnp.int32, (DH, DH), axis) for axis in range(2))
    weights = jnp.concatenate([b_ref[:depth, :], f_ref[:depth, :]], axis=0)
    for place, ref in enumerate((mine_ref, theirs_ref)):
        whole = (acc_ref[place, 0] + jnp.dot(ref[...], weights, preferred_element_type=F32)).astype(BF16)
        q_ref[place] = whole
        columns = jnp.transpose(decay_ref[place])
        for start in range(0, rows, DH):
            stop = start + DH
            for h in range(width // DH):
                cut = slice(h * DH, (h + 1) * DH)
                q = whole[start:stop, cut]
                column, row = columns[start:stop, h : h + 1], decay_ref[place, h : h + 1, :stop]
                raw = lax.dot_general(q, kv_ref[place, 0, :stop, cut], ACROSS, preferred_element_type=F32) * scale
                gap = jnp.where(i >= j, column - row[:, start:], -1e30)
                scores = (raw[:, start:] * jnp.exp(gap)).astype(BF16)
                if start:
                    border = row[:, start - 1 : start]
                    faded = raw[:, :start] * jnp.exp(column - border) * jnp.exp(border - row[:, :start])
                    scores = jnp.concatenate([faded.astype(BF16), scores], axis=1)
                out_ref[place, start:stop, cut] = jnp.dot(
                    scores, kv_ref[place, 1, :stop, cut], preferred_element_type=F32
                )


def inter_body(scale, q_ref, decay_ref, intra_ref, state_ref, out_ref, square_ref):
    rows, width = q_ref.shape[1:]
    squares = jnp.zeros((8, rows), F32)
    grown = jnp.transpose(jnp.exp(decay_ref[0]) * scale)
    for h in range(width // DH):
        cut = slice(h * DH, (h + 1) * DH)
        q = q_ref[0, :, cut]
        inter = jnp.dot(jnp.concatenate([q] * 3, axis=1), state_ref[0, h], preferred_element_type=F32)
        attended = intra_ref[0, :, cut] + inter * grown[:, h : h + 1]
        out_ref[0, :, cut] = attended
        for part in split(attended * attended, 2):
            squares += lax.dot_general(jnp.ones((8, DH), BF16), part.astype(BF16), ACROSS, preferred_element_type=F32)
    square_ref[0] = squares


def by_place(body, outs, flops, *args):
    def whole(shape):
        return pl.BlockSpec((1,) + shape[1:], lambda a: (a,) + (0,) * (len(shape) - 1))

    return pl.pallas_call(
        functools.partial(body, DH**-0.5),
        out_shape=[jax.ShapeDtypeStruct(shape, F32) for shape in outs],
        grid=(2,),
        in_specs=[whole(arg.shape) for arg in args],
        out_specs=[whole(shape) for shape in outs],
        compiler_params=pltpu.CompilerParams(vmem_limit_bytes=VMEM_LIMIT),
        cost_estimate=pl.CostEstimate(flops=flops, bytes_accessed=4 * 10**6, transcendentals=10**6),
    )(*args)


def on_device(tokens, w_qkv, log_decay, gain):
    rows = tokens.shape[0]
    width = w_qkv.shape[2] // 2
    group = width // DH
    x, z, core = lax.axis_index("x"), lax.axis_index("zl"), lax.axis_index("core")
    place = core.reshape(1)

    def halves(array, axis):
        size = array.shape[axis] // 2
        mine = lax.dynamic_slice_in_dim(array, core * size, size, axis)
        theirs = lax.dynamic_slice_in_dim(array, (1 - core) * size, size, axis)
        return mine, theirs

    kept, sent = halves(w_qkv, 2)
    got = lax.ppermute(sent, "core", SWAP)
    own = jnp.where(core == 0, jnp.concatenate([kept, got], 1), jnp.concatenate([got, kept], 1))
    kept, sent = halves(log_decay, 0)
    decay = jnp.stack([kept, lax.ppermute(tied(sent, own), "core", SWAP)])
    other_tokens = lax.ppermute(tied(tokens, own), "core", SWAP)

    fades = jnp.pad(jnp.cumsum(decay, axis=2), ((0, 0), (0, 8 - group), (0, 0)))

    columns = [x, (x + 3) % 4, (x + 1) % 4, (x + 2) % 4]
    index = [[(4 * c + (z + 4 - d) % 4).astype(jnp.int32) for d in range(4)] for c in columns]
    own_x, right_x, left_x, far_x = index

    def along_z(part):
        return lax.ppermute(part, "zl", NEXT)

    def to_right(part):
        return lax.ppermute(part, "x", NEXT)

    def to_left(part):
        return lax.ppermute(part, "x", LAST)

    def tokens_at(array, chunks):
        return jnp.concatenate([lax.dynamic_slice_in_dim(array, c * depth, depth, 1) for c in chunks], axis=1)

    step = lax.optimization_barrier
    depth = own.shape[1]
    own = own.reshape(-1, width)
    half = own.shape[0] // 2
    a1, r0, l0 = along_z(own), to_right(own), to_left(own)

    a2, r1, l1, f0, g0 = along_z(a1), to_right(a1), to_left(a1), to_right(r0[:half]), to_left(l0[half:])

    held = tied(a2, r1, l1, f0, g0)
    a3, r2, l2 = along_z(held), to_right(held), to_left(held)

    far0 = jnp.concatenate([f0, g0])
    sent_z, sent_x = tied((far0, a3), r2, l2)
    b1, r3, l3 = along_z(sent_z), to_right(sent_x), to_left(sent_x)
    chunks = [own_x[0], own_x[1], right_x[0], left_x[0], own_x[2], right_x[1], left_x[1], far_x[0]]
    acc = project(chunks, tokens, other_tokens, [own, a1, r0, l0, a2, r1, l1, far0], None)
    last = [tokens_at(array, (far_x[2], far_x[3])) for array in (tokens, other_tokens)]

    sent_z, sent_r, sent_l, last = tied((b1, r3, l3, last), a3, r2, l2, acc, fades)
    b2, f3, g3 = along_z(sent_z), to_right(sent_r[:half]), to_left(sent_l[half:])
    chunks = [own_x[3], right_x[2], left_x[2], far_x[1], right_x[3], left_x[3]]
    q_acc, kv_acc = project(chunks, tokens, other_tokens, [a3, r2, l2, b1, r3, l3], acc)
    b2, f3, g3, q_acc, kv_acc = step((b2, f3, g3, q_acc, kv_acc))

    shape = (group, DH + TAIL, DH)
    outs = [((2, 2, rows, width), BF16), (shape, F32), (shape, BF16), (shape, F32)]
    kv, chip, sent, first = small_kernel(close_body, outs, place, *last, b2, f3, g3, kv_acc, fades)
    backs = [lax.ppermute(sent, "zl", [(i, (i + j) % 4) for i in range(4)]) for j in (1, 2, 3)]
    outs = [((2, rows, width), BF16), ((2, rows, width), F32)]
    q, intra = small_kernel(functools.partial(intra_body, DH**-0.5), outs, place, *last, b2, f3, q_acc, kv, fades)
    backs, intra = step((backs, intra))
    before, row = small_kernel(row_body, [(shape, F32), (shape, BF16)], z.reshape(1), chip, *backs)
    backs = [lax.ppermute(row, "x", [(i, (i + j) % 4) for i in range(4)]) for j in (1, 2, 3)]
    (state,) = small_kernel(incoming_body, [((2, group, 3 * DH, DH), BF16)], jnp.stack([core, x]), before, first, *backs)

    attended, squares = by_place(inter_body, [(2, rows, width), (2, 8, rows)], 10**9, q, fades, intra, state)
    squares = squares[:, 0, :]
    summed = squares[0] + lax.ppermute(squares[1], "core", SWAP)
    got = lax.ppermute(tied(attended[1], summed), "core", SWAP)
    summed = summed + sum(lax.ppermute(summed, "y", [(i, (i + j) % 4) for i in range(4)]) for j in (1, 2, 3))
    summed = summed + lax.ppermute(summed, "zh", SWAP)
    scale = lax.rsqrt(summed / (HEAD_COUNT * DH) + 1e-6)[:, None]
    mine = attended[0]
    whole = jnp.where(core == 0, jnp.concatenate([mine, got], 1), jnp.concatenate([got, mine], 1))
    return (whole * scale * gain[None, :]).astype(BF16)


def solution(mesh):
    fine = Mesh(mesh.devices.reshape(4, 4, 2, 4, 2), ("x", "zl", "core", "y", "zh"))
    seq, head = ("x", "zl", "core"), ("y", "zh")
    return jax.shard_map(
        on_device,
        mesh=fine,
        in_specs=(P(seq, None), P(None, seq, head), P(head, seq), P(head)),
        out_specs=P(seq, head),
        check_vma=False,
    )
```
